256 devices in a mesh: ctx: 16 (over z, core), tp: 16 (over x, y).
Axes of the slice: x: 4, y: 4, z: 8, core: 2. Of those that a mesh axis runs over, the one named last changes fastest.
Arguments:
- tokens: bfloat16 [4096, 4096], P('ctx', 'tp'), may hold values from -6 to 6
- w_z: bfloat16 [4096, 8192], P(None, 'tp'), may hold values from -0.09375 to 0.09375
- w_x: bfloat16 [4096, 8192], P(None, 'tp'), may hold values from -0.09375 to 0.09375
- w_bc: bfloat16 [4096, 2048], P(None, 'tp'), may hold values from -0.09375 to 0.09375
- conv_x: float32 [4, 8192], P(None, 'tp'), may hold values from -3 to 3
- conv_bc: float32 [4, 2048], P(None, 'tp'), may hold values from -3 to 3
- bias_x: float32 [8192], P('tp'), may hold values from -0.5 to 0.5
- bias_bc: float32 [2048], P('tp'), may hold values from -0.5 to 0.5
- decay_logarithm: float32 [4096, 128], P('ctx', 'tp'), may hold values from -1.3 to 0, as said below
- head_step: float32 [128], P('tp'), may hold values from 0 to 0.3, as said below
- skip: float32 [128], P('tp'), may hold values from 0.5 to 1.5
- gain: float32 [8192], P('tp'), may hold values from 0.5 to 1.5
Outputs:
- normed: bfloat16 [4096, 8192], P('ctx', 'tp')
The draws below stay inside these ranges and needn't reach their ends.
Inputs may be any that keep to these rules, and one draw needn't show every extreme that they name: decay_logarithm is negative. head_step is positive.
All inputs are finite; a program needn't handle non-finite values.
Results may differ from the reference program's by a relative error of at most 0.0095.
Values may be sent and summed in bfloat16 or wider, within the bound.
A program may use at most 64 MiB of HBM per device.

```python
import jax
import jax.numpy as jnp
from jax import lax

D = 4096
P_SIZE = 64
N = 128
KERNEL = 4
STRETCH = 256
TOK_DEV = 256
HEADS = 128
GROUP_HEADS = 16
GROUPS = 8
D_INNER = 8192
TOKENS = 4096


def head_rates(key):
    base_key = jax.random.fold_in(key, 11)
    pick_key, slow_key, quick_key = jax.random.split(base_key, 3)
    fast_share = 0.5
    quick_heads = jax.random.bernoulli(pick_key, fast_share, (HEADS,))
    slow_rate = jnp.exp(jax.random.uniform(slow_key, (HEADS,), jnp.float32, jnp.log(0.05), jnp.log(0.5))) / TOKENS
    quick_rate = jnp.exp(jax.random.uniform(quick_key, (HEADS,), jnp.float32, jnp.log(1.0 / 50.0), jnp.log(1.0 / 30.0)))
    return jnp.where(quick_heads, quick_rate, slow_rate)


def draw_head_step(key, part):
    rates = head_rates(key)
    return (1.5 * jnp.sqrt(rates)).astype(jnp.float32)


def draw_decay_logarithm(key, part):
    rates = head_rates(key)
    own_key = jax.random.fold_in(key, 23)
    block_key, token_key, place_key, loss_key = jax.random.split(own_key, 4)
    block_total = TOKENS // TOK_DEV
    block_factor = jnp.exp(jax.random.uniform(block_key, (block_total, HEADS), jnp.float32, jnp.log(0.5), jnp.log(2.0)))
    token_factor = jnp.exp(jax.random.uniform(token_key, (TOKENS, HEADS), jnp.float32, jnp.log(0.7), jnp.log(1.4)))
    factor = jnp.repeat(block_factor, TOK_DEV, axis=0) * token_factor
    constant_rate = -rates[None, :] * factor
    token_places = jax.random.randint(place_key, (2, HEADS), 0, TOKENS)
    error_values = jax.random.uniform(loss_key, (2, HEADS), jnp.float32, 0.2, 0.45)
    token_positions = jnp.arange(TOKENS)[:, None]
    token_runs = jnp.where(token_positions == token_places[0][None, :], jnp.log1p(-error_values[0])[None, :], 0.0)
    token_runs = token_runs + jnp.where(token_positions == token_places[1][None, :], jnp.log1p(-error_values[1])[None, :], 0.0)
    return (constant_rate + token_runs).astype(jnp.float32)


def block_levels(rng, dims, cuts, least, largest):
    factor_of = 1.0
    for position, parts in cuts:
        draws = jax.random.uniform(jax.random.fold_in(jax.random.fold_in(rng, 6), position), (parts,), jnp.float32, least / len(cuts), largest / len(cuts))
        factor_of = factor_of * jnp.repeat(jnp.exp(draws), dims[position] // parts).reshape((-1,) + (1,) * (len(dims) - 1 - position))
    return factor_of


def centred(key, dims, scale, most, shards=(), kind=jnp.bfloat16):
    factor_of = block_levels(key, dims, shards, -0.22, 0.18) if shards else 1.0
    drawn = jax.random.normal(key, dims, jnp.float32) * scale * factor_of
    return jnp.minimum(jnp.maximum(drawn, -most), most).astype(kind)


def setup_inputs(seed: int = 0) -> dict:
    seeds = jax.random.split(jax.random.key(seed), 13)
    tokens = centred(seeds[0], (TOKENS, D), 1.0, 6.0, ((0, 16), (1, 16)))
    w_z = centred(seeds[1], (D, D_INNER), D ** -0.5, 0.09375, ((1, 16),))
    w_x = centred(seeds[2], (D, D_INNER), D ** -0.5, 0.09375, ((1, 16),))
    w_bc = centred(seeds[3], (D, 2 * GROUPS * N), D ** -0.5, 0.09375, ((1, 16),))
    conv_x = centred(seeds[4], (KERNEL, D_INNER), KERNEL ** -0.5, 3.0, ((1, 16),), jnp.float32)
    conv_bc = centred(seeds[5], (KERNEL, 2 * GROUPS * N), KERNEL ** -0.5, 3.0, ((1, 16),), jnp.float32)
    bias_x = jnp.clip(jax.random.uniform(seeds[6], (D_INNER,), jnp.float32, -0.5, 0.5) * block_levels(seeds[6], (D_INNER,), ((0, 16),), -0.4, 0.0), -0.5, 0.5)
    bias_bc = jnp.clip(jax.random.uniform(seeds[7], (2 * GROUPS * N,), jnp.float32, -0.5, 0.5) * block_levels(seeds[7], (2 * GROUPS * N,), ((0, 16),), -0.4, 0.0), -0.5, 0.5)
    decay_logarithm = draw_decay_logarithm(jax.random.fold_in(seeds[12], 71), 0)
    head_step = draw_head_step(jax.random.fold_in(seeds[12], 71), 0)
    skip = jnp.clip(0.5 + 1.0 * jax.random.uniform(seeds[10], (HEADS,), jnp.float32) ** block_levels(seeds[10], (HEADS,), ((0, 16),), -0.2, 0.2), 0.5, 1.5)
    gain = jnp.clip(1.0 + 0.1 * jax.random.normal(seeds[11], (D_INNER,), jnp.float32), 0.5, 1.5)
    return dict(tokens=tokens, w_z=w_z, w_x=w_x, w_bc=w_bc, conv_x=conv_x, conv_bc=conv_bc, bias_x=bias_x, bias_bc=bias_bc, decay_logarithm=decay_logarithm, head_step=head_step, skip=skip, gain=gain)


def causal_conv(pre_conv, taps, offset_bias):
    width = pre_conv.shape[1]
    extended = jnp.concatenate([jnp.zeros((KERNEL - 1, width), jnp.float32), pre_conv.astype(jnp.float32)], axis=0)
    total = offset_bias[None, :] + jnp.zeros((TOKENS, width), jnp.float32)
    for offset in range(KERNEL):
        total = total + taps[offset][None, :] * extended[offset:offset + TOKENS]
    return jax.nn.silu(total).astype(jnp.bfloat16)

def group_scan(inputs):
    x_group, decay_group, b_group, c_group, step_group = inputs
    stretch_count = TOKENS // STRETCH
    x_blocks = x_group.astype(jnp.float32).reshape(stretch_count, STRETCH, GROUP_HEADS, P_SIZE)
    decay_blocks = decay_group.reshape(stretch_count, STRETCH, GROUP_HEADS)
    b_blocks = b_group.astype(jnp.float32).reshape(stretch_count, STRETCH, N)
    c_blocks = c_group.astype(jnp.float32).reshape(stretch_count, STRETCH, N)
    causal = jnp.tril(jnp.ones((STRETCH, STRETCH), dtype=bool))[:, :, None]

    def one_block(state, block):
        x_block, decay_block, b_block, c_block = block
        cum_decay = jnp.cumsum(decay_block, axis=0)
        pair_diff = cum_decay[:, None, :] - cum_decay[None, :, :]
        segment = jnp.where(causal, jnp.exp(jnp.where(causal, pair_diff, 0.0)), 0.0)
        scores = jnp.dot(c_block, b_block.T, precision=lax.Precision.HIGHEST)
        mixing = segment * scores[:, :, None] * step_group
        intra_out = jnp.einsum('ijh,jhp->ihp', mixing, x_block, precision=lax.Precision.HIGHEST)
        inter_out = jnp.einsum('in,hpn->ihp', c_block, state, precision=lax.Precision.HIGHEST) * jnp.exp(cum_decay)[:, :, None]
        end_weight = jnp.exp(cum_decay[-1][None, :] - cum_decay) * step_group
        added = jnp.einsum('jh,jhp,jn->hpn', end_weight, x_block, b_block, precision=lax.Precision.HIGHEST)
        new_state = jnp.exp(cum_decay[-1])[:, None, None] * state + added
        return (new_state, intra_out + inter_out)
    start_state = jnp.zeros((GROUP_HEADS, P_SIZE, N), jnp.float32)
    _, outputs = lax.scan(one_block, start_state, (x_blocks, decay_blocks, b_blocks, c_blocks))
    return outputs.reshape(TOKENS, GROUP_HEADS, P_SIZE)

def reference(tokens, w_z, w_x, w_bc, conv_x, conv_bc, bias_x, bias_bc, decay_logarithm, head_step, skip, gain):
    gate_in = jnp.dot(tokens, w_z, preferred_element_type=jnp.float32).astype(jnp.bfloat16)
    x_pre = jnp.dot(tokens, w_x, preferred_element_type=jnp.float32).astype(jnp.bfloat16)
    bc_pre = jnp.dot(tokens, w_bc, preferred_element_type=jnp.float32).astype(jnp.bfloat16)
    x_conv = causal_conv(x_pre, conv_x, bias_x)
    bc_conv = causal_conv(bc_pre, conv_bc, bias_bc).reshape(TOKENS, GROUPS, 2, N)
    b_all = jnp.transpose(bc_conv[:, :, 0, :], (1, 0, 2))
    c_all = jnp.transpose(bc_conv[:, :, 1, :], (1, 0, 2))
    x_groups = jnp.transpose(x_conv.reshape(TOKENS, GROUPS, GROUP_HEADS, P_SIZE), (1, 0, 2, 3))
    decay_groups = jnp.transpose(decay_logarithm.reshape(TOKENS, GROUPS, GROUP_HEADS), (1, 0, 2))
    step_groups = head_step.reshape(GROUPS, GROUP_HEADS)
    scanned = lax.map(group_scan, (x_groups, decay_groups, b_all, c_all, step_groups))
    scanned = jnp.transpose(scanned, (1, 0, 2, 3)).reshape(TOKENS, HEADS, P_SIZE)
    head_out = scanned + skip[None, :, None] * x_conv.astype(jnp.float32).reshape(TOKENS, HEADS, P_SIZE)
    gated = head_out.reshape(TOKENS, D_INNER) * jax.nn.silu(gate_in.astype(jnp.float32))
    grouped = gated.reshape(TOKENS, GROUPS, GROUP_HEADS * P_SIZE)
    mean_square = lax.optimization_barrier(jnp.mean(grouped * grouped, axis=2))
    scaled = grouped * lax.rsqrt(mean_square + 1e-05)[:, :, None]
    return (scaled.reshape(TOKENS, D_INNER) * gain[None, :]).astype(jnp.bfloat16)
```

```python
import jax
import jax.numpy as jnp
from jax import lax
from jax.experimental import pallas as pl
from jax.experimental.pallas import tpu as pltpu
from jax.sharding import PartitionSpec as P

MESH = pl.DeviceIdType.MESH
SIDE = 4
TAPS = 4
ROWS = 256
HALF = 128
FEAT = 256
SECTIONS = 16
LT = 4
F32 = jnp.float32
BF16 = jnp.bfloat16


def silu(v):
    return v / (1.0 + jnp.exp(-v))


def dot(a, b, **kw):
    return jnp.dot(a, b, preferred_element_type=F32, **kw)


def kernel(
    tok, wz, wx, wbc, conv_x, conv_bc, bias_x, bias_bc, decay_t, step, skip, gain, out,
    held, vz, vx, vbc, acc_z, acc_x, acc_bc, pre, rim_out, rim_in, xs, bc, seg, grow, end_w,
    tot_out, tot_in, st_out, st_in, en_out, en_in, y, sq_out, sq_in,
    w_sem, own_sem, g_send, g_recv, tot_send, tot_recv, rim_sem, bc_sem, st_sem, en_sem, sq_sem,
):
    ctx, tp = lax.axis_index("ctx"), lax.axis_index("tp")
    core = lax.rem(ctx, 2)
    x, y_at = lax.div(tp, SIDE), lax.rem(tp, SIDE)

    def at(px, py):
        return lax.rem(px + 2 * SIDE, SIDE) * SIDE + lax.rem(py + 2 * SIDE, SIDE)

    mate = at(x, y_at + 1 - 2 * lax.rem(y_at, 2))
    later = lax.rem(ctx + 1, SECTIONS)

    barrier = pltpu.get_barrier_semaphore()
    for px, py in ((1, 0), (-1, 0), (0, 1), (0, -1)):
        pl.semaphore_signal(
            barrier, inc=1, device_id=(ctx, at(x + px, y_at + py)), device_id_type=MESH
        )

    def greet(i, c):
        other = lax.rem(ctx + i, SECTIONS)
        pl.semaphore_signal(barrier, inc=1, device_id=(other, tp), device_id_type=MESH)
        return c

    lax.fori_loop(1, SECTIONS, greet, 0)

    weights = [
        pltpu.make_async_copy(a, b, w_sem.at[i])
        for i, (a, b) in enumerate(((wx, vx), (wbc, vbc), (wz, vz)))
    ]
    own = pltpu.make_async_copy(tok, held.at[tp], own_sem)
    own.start()
    for w in weights:
        w.start()
    pl.semaphore_wait(barrier, 4 + SECTIONS - 1)

    def slot(dx, dy):
        return at(x - dx, y_at - dy)

    def piece(s, half):
        return held.at[s, pl.ds(half * HALF, HALF), :]

    def dxy(half, first, second):
        return (second, first) if half == 0 else (first, second)

    def send(half, source, direction, along, landing):
        dx, dy = dxy(half, *source)
        px, py = dxy(half, *((direction, 0) if along == 0 else (0, direction)))
        first, second = landing
        s = slot(dx, dy)
        src = tok.at[pl.ds(half * HALF, HALF), :] if all(isinstance(v, int) and v == 0 for v in source) else piece(s, half)
        pltpu.make_async_remote_copy(
            src_ref=src,
            dst_ref=piece(s, half),
            send_sem=g_send,
            recv_sem=g_recv.at[half, first * SIDE + second],
            device_id=(ctx, at(x + px, y_at + py)),
            device_id_type=MESH,
        ).start()

    def arrived(half, first, second):
        p = piece(slot(*dxy(half, first, second)), half)
        pltpu.make_async_copy(p, p, g_recv.at[half, first * SIDE + second]).wait()

    def along_second(half, first):
        send(half, (first, 0), 1, 1, (first, 1))
        send(half, (first, 0), -1, 1, (first, 3))

    def across_second(half, first):
        flag = lax.rem(first + core, 2)
        send(half, (first, 1 + 2 * flag), 1 - 2 * flag, 1, (first, 2))

    def multiply(dx, dy, begin=False):
        s = slot(dx, dy)
        a = held[s]
        depth = pl.ds(pl.multiple_of(s * FEAT, FEAT), FEAT)
        for acc, v in ((acc_x, vx), (acc_bc, vbc), (acc_z, vz)):
            part = dot(a, v[depth, :])
            acc[...] = part if begin else acc[...] + part

    def multiply_all(count, offsets):
        def body(i, c):
            multiply(*offsets(i))
            return c

        lax.fori_loop(0, count, body, 0)

    for half in (0, 1):
        send(half, (0, 0), 1, 0, (1, 0))
        send(half, (0, 0), -1, 0, (3, 0))
    for half in (0, 1):
        along_second(half, 0)

    i0 = lax.broadcasted_iota(jnp.int32, (ROWS, ROWS), 0)
    i1 = lax.broadcasted_iota(jnp.int32, (ROWS, ROWS), 1)
    upper = (i0 <= i1).astype(F32)
    cum_t = dot(decay_t[...], upper, precision=lax.Precision.HIGHEST)
    lane = lax.broadcasted_iota(jnp.int32, (1, 128), 1)
    for t in range(LT):
        rows = jnp.concatenate(
            [jnp.broadcast_to(cum_t[2 * t + k : 2 * t + k + 1], (64, ROWS)) for k in (0, 1)], 0
        )
        cum = rows.T
        total = cum[ROWS - 1 : ROWS]
        step_row = jnp.where(lane < 64, step[2 * t], step[2 * t + 1])
        grow[t] = jnp.exp(cum)
        end_w[t] = jnp.exp(total - cum) * step_row
        tot_out[t] = jnp.broadcast_to(jnp.exp(total), (8, 128))

    my_tile = lax.div(ctx, 4)
    tot_in[ctx] = tot_out[my_tile]

    def send_total(i, c):
        o = lax.rem(ctx + i, SECTIONS)
        pltpu.make_async_remote_copy(
            src_ref=tot_out.at[lax.div(o, 4)],
            dst_ref=tot_in.at[ctx],
            send_sem=tot_send,
            recv_sem=tot_recv,
            device_id=(o, tp),
            device_id_type=MESH,
        ).start()
        return c

    lax.fori_loop(1, SECTIONS, send_total, 0)

    for half in (0, 1):
        arrived(half, 1, 0)
        arrived(half, 3, 0)
        send(half, (1 + 2 * core, 0), 1 - 2 * core, 0, (2, 0))
        along_second(half, 1)
        along_second(half, 3)
    for h in range(8):
        if h == 4:
            for half in (0, 1):
                arrived(half, 0, 1)
                arrived(half, 0, 3)
                across_second(half, 0)
        row = cum_t[h : h + 1]
        col = jnp.broadcast_to(row, (128, ROWS)).T
        col = jnp.concatenate([col, col], axis=1)
        keep = i0 >= i1
        seg[h] = jnp.where(keep, jnp.exp(jnp.where(keep, col - row, 0.0)), 0.0) * step[h]

    for half in (0, 1):
        arrived(half, 2, 0)
        along_second(half, 2)
    own.wait()
    for w in weights:
        w.wait()
    multiply(0, 0, True)

    def beside(i):
        o, swap = 1 + 2 * lax.rem(i, 2), lax.div(i, 2)
        return swap * o, (1 - swap) * o

    multiply_all(4, beside)
    for half in (0, 1):
        for first in (1, 3):
            arrived(half, first, 1)
            arrived(half, first, 3)
            across_second(half, first)
    multiply_all(4, lambda i: (1 + 2 * lax.rem(i, 2), 1 + 2 * lax.div(i, 2)))
    for half in (0, 1):
        arrived(half, 0, 2)
        arrived(half, 2, 1)
        arrived(half, 2, 3)
        across_second(half, 2)
    multiply_all(2, lambda i: (2 * (1 - i), 2 * i))
    for half in (0, 1):
        arrived(half, 1, 2)
        arrived(half, 3, 2)

    def far(i):
        o, swap = 1 + 2 * lax.rem(i, 2), lax.div(i, 2)
        return o + swap * (2 - o), 2 + swap * (o - 2)

    multiply_all(4, far)
    for half in (0, 1):
        arrived(half, 2, 2)
    multiply(2, 2)

    for t in range(LT + 1):
        p = acc_bc[...] if t == LT else acc_x[:, t * 128 : (t + 1) * 128]
        p = p.astype(BF16)
        rim_out[t] = p[ROWS - 16 :]
        pre[t, 8 : 8 + ROWS] = p.astype(F32)
    rim = pltpu.make_async_remote_copy(
        src_ref=rim_out,
        dst_ref=rim_in,
        send_sem=rim_sem.at[0],
        recv_sem=rim_sem.at[1],
        device_id=(later, tp),
        device_id_type=MESH,
    )
    rim.start()
    rim.wait_recv()

    def conv(t):
        pre[t, 0:8] = jnp.where(ctx > 0, rim_in[t].astype(F32)[8:], 0.0)
        cols = slice(0, 128) if t == LT else slice(t * 128, (t + 1) * 128)
        taps, bias = (conv_bc, bias_bc) if t == LT else (conv_x, bias_x)
        total = bias[:, cols] + jnp.zeros((ROWS, 128), F32)
        for k in range(TAPS):
            total = total + taps[k : k + 1, cols] * pre[t, 5 + k : 5 + k + ROWS]
        return silu(total).astype(BF16)

    side = lax.rem(tp, 2)
    bc[side] = conv(LT)
    swap = pltpu.make_async_remote_copy(
        src_ref=bc.at[side],
        dst_ref=bc.at[side],
        send_sem=bc_sem.at[0],
        recv_sem=bc_sem.at[1],
        device_id=(ctx, mate),
        device_id_type=MESH,
    )
    swap.start()
    for t in range(LT):
        xs[t] = conv(t)
    other = bc.at[1 - side]
    pltpu.make_async_copy(other, other, bc_sem.at[1]).wait()

    b_t = bc[0].astype(F32).T.astype(BF16)
    for t in range(LT):
        weighted = (xs[t].astype(F32) * end_w[t]).astype(BF16)
        st_out[4 * t : 4 * t + 4] = dot(b_t, weighted).reshape(4, 32, 128).astype(BF16)
    st_in[ctx] = st_out[ctx]

    def send_state(i, c):
        o = lax.rem(ctx + i, SECTIONS)
        pltpu.make_async_remote_copy(
            src_ref=st_out.at[o],
            dst_ref=st_in.at[ctx],
            send_sem=st_sem.at[0],
            recv_sem=st_sem.at[1],
            device_id=(o, tp),
            device_id_type=MESH,
        ).start()
        return c

    lax.fori_loop(1, SECTIONS, send_state, 0)

    scores = dot(bc[1], b_t)

    def intra(t):
        both = [dot((seg[2 * t + k] * scores).astype(BF16), xs[t]) for k in (0, 1)]
        skip_row = jnp.where(lane < 64, skip[2 * t], skip[2 * t + 1])
        y[t] = jnp.where(lane < 64, both[0], both[1]) + skip_row * xs[t].astype(F32)

    for t in range(2):
        intra(t)

    def all_but_one(ref, sem):
        part = ref.at[pl.ds(0, SECTIONS - 1)]
        pltpu.make_async_copy(part, part, sem).wait()

    all_but_one(tot_in, tot_recv)
    all_but_one(st_in, st_sem.at[1])
    state = jnp.zeros((32, 128), F32)
    for s in range(SECTIONS):
        en_out[s] = state.astype(BF16)
        state = tot_in[s][0:1] * state + st_in[s].astype(F32)
    en_in[ctx] = en_out[ctx]

    def send_entering(i, c):
        o = lax.rem(ctx + i, SECTIONS)
        pltpu.make_async_remote_copy(
            src_ref=en_out.at[o],
            dst_ref=en_in.at[ctx],
            send_sem=en_sem.at[0],
            recv_sem=en_sem.at[1],
            device_id=(o, tp),
            device_id_type=MESH,
        ).start()
        return c

    lax.fori_loop(1, SECTIONS, send_entering, 0)
    for t in range(2, LT):
        intra(t)
    for t in range(LT):
        g = acc_z[:, t * 128 : (t + 1) * 128].astype(BF16).astype(F32)
        acc_z[:, t * 128 : (t + 1) * 128] = silu(g)
    all_but_one(en_in, en_sem.at[1])

    squares = jnp.zeros((ROWS, 128), F32)
    for t in range(LT):
        entering = en_in[4 * t : 4 * t + 4].reshape(128, 128)
        gated = (y[t] + grow[t] * dot(bc[1], entering)) * acc_z[:, t * 128 : (t + 1) * 128]
        squares = squares + gated * gated
        y[t] = gated
    local = jnp.sum(squares.T, axis=0, keepdims=True)
    sq_out[...] = jnp.broadcast_to(local, (8, ROWS))
    norm = pltpu.make_async_remote_copy(
        src_ref=sq_out,
        dst_ref=sq_in,
        send_sem=sq_sem.at[0],
        recv_sem=sq_sem.at[1],
        device_id=(ctx, mate),
        device_id_type=MESH,
    )
    norm.start()
    norm.wait_recv()
    mean = (sq_out[0:1] + sq_in[0:1]) * (1.0 / (2 * LT * 128))
    scale = jnp.broadcast_to(lax.rsqrt(mean + 1e-5), (128, ROWS)).T
    for t in range(LT):
        cols = slice(t * 128, (t + 1) * 128)
        out[:, cols] = (y[t] * scale * gain[:, cols]).astype(BF16)

    norm.wait_send()
    rim.wait_send()
    swap.wait_send()
    all_but_one(held, g_send)
    all_but_one(tot_in, tot_send)
    all_but_one(st_out, st_sem.at[0])
    all_but_one(en_out, en_sem.at[0])


def local(tokens, w_z, w_x, w_bc, conv_x, conv_bc, bias_x, bias_bc, decay, step, skip, gain):
    hbm = pl.BlockSpec(memory_space=pl.ANY)
    vmem = pl.BlockSpec(memory_space=pltpu.VMEM)
    smem = pl.BlockSpec(memory_space=pltpu.SMEM)
    width = w_x.shape[1]
    dma = pltpu.SemaphoreType.DMA
    scratch = [
        pltpu.VMEM((16, ROWS, FEAT), BF16),
        pltpu.VMEM(w_z.shape, BF16),
        pltpu.VMEM(w_x.shape, BF16),
        pltpu.VMEM(w_bc.shape, BF16),
        pltpu.VMEM((ROWS, width), F32),
        pltpu.VMEM((ROWS, width), F32),
        pltpu.VMEM((ROWS, 128), F32),
        pltpu.VMEM((LT + 1, 8 + ROWS, 128), F32),
        pltpu.VMEM((LT + 1, 16, 128), BF16),
        pltpu.VMEM((LT + 1, 16, 128), BF16),
        pltpu.VMEM((LT, ROWS, 128), BF16),
        pltpu.VMEM((2, ROWS, 128), BF16),
        pltpu.VMEM((8, ROWS, ROWS), F32),
        pltpu.VMEM((LT, ROWS, 128), F32),
        pltpu.VMEM((LT, ROWS, 128), F32),
        pltpu.VMEM((LT, 8, 128), F32),
        pltpu.VMEM((SECTIONS, 8, 128), F32),
        pltpu.VMEM((SECTIONS, 32, 128), BF16),
        pltpu.VMEM((SECTIONS, 32, 128), BF16),
        pltpu.VMEM((SECTIONS, 32, 128), BF16),
        pltpu.VMEM((SECTIONS, 32, 128), BF16),
        pltpu.VMEM((LT, ROWS, 128), F32),
        pltpu.VMEM((8, ROWS), F32),
        pltpu.VMEM((8, ROWS), F32),
        dma((3,)),
        dma,
        dma,
        dma((2, 16)),
        dma,
        dma,
        dma((2,)),
        dma((2,)),
        dma((2,)),
        dma((2,)),
        dma((2,)),
    ]
    return pl.pallas_call(
        kernel,
        out_shape=jax.ShapeDtypeStruct((ROWS, width), BF16),
        in_specs=[hbm] * 4 + [vmem] * 5 + [smem] * 2 + [vmem],
        out_specs=vmem,
        scratch_shapes=scratch,
        compiler_params=pltpu.CompilerParams(
            collective_id=0, has_side_effects=True, vmem_limit_bytes=56 * 2**20
        ),
    )(
        tokens, w_z, w_x, w_bc, conv_x, conv_bc, bias_x.reshape(1, -1), bias_bc.reshape(1, -1),
        decay.T, step, skip, gain.reshape(1, -1),
    )


def solution(mesh):
    return jax.shard_map(
        local,
        mesh=mesh,
        in_specs=(
            P("ctx", "tp"),
            P(None, "tp"),
            P(None, "tp"),
            P(None, "tp"),
            P(None, "tp"),
            P(None, "tp"),
            P("tp"),
            P("tp"),
            P("ctx", "tp"),
            P("tp"),
            P("tp"),
            P("tp"),
        ),
        out_specs=P("ctx", "tp"),
        check_vma=False,
    )
```

```python
import jax
import jax.numpy as jnp
from jax import lax
from jax.experimental import pallas as pl
from jax.experimental.pallas import tpu as pltpu
from jax.sharding import PartitionSpec as P

MESH = pl.DeviceIdType.MESH
SIDE = 4
TAPS = 4
ROWS = 256
HALF = 128
FEAT = 256
SECTIONS = 16
PEERS = 8
SLICE = 64
LT = 4
F32 = jnp.float32
BF16 = jnp.bfloat16


def silu(v):
    return v / (1.0 + jnp.exp(-v))


def dot(a, b, **kw):
    return jnp.dot(a, b, preferred_element_type=F32, **kw)


def kernel(
    tok, wz, wx, wbc, conv_x, conv_bc, bias_x, bias_bc, decay_t, step, skip, gain, out,
    held, vz, vx, vbc, acc_z, acc_x, acc_bc, pre, rim_out, rim_in, xs, bc, seg, grow, end_w,
    tot_out, tot_in, st_out, st_in, en_out, en_in, half_out, half_in, y, sq_out, sq_in,
    w_sem, own_sem, g_send, g_recv, tot_send, tot_recv, rim_sem, bc_sem, st_send, st_recv,
    en_send, en_recv, half_sem, sq_sem, up, down, facing,
):
    ctx, tp = lax.axis_index("ctx"), lax.axis_index("tp")
    core = lax.rem(ctx, 2)
    x, y_at = lax.div(tp, SIDE), lax.rem(tp, SIDE)

    def at(px, py):
        return lax.rem(px + 2 * SIDE, SIDE) * SIDE + lax.rem(py + 2 * SIDE, SIDE)

    mate = at(x, y_at + 1 - 2 * lax.rem(y_at, 2))
    z = lax.div(ctx, 2)
    group, me = lax.div(ctx, PEERS), lax.rem(ctx, PEERS)
    place = lax.rem(z, 4)
    mirror = (7 - z) * 2 + core

    def owner(o):
        p = lax.div(o, 2)
        return (p + group * (3 - 2 * p)) * 2 + lax.rem(o, 2)

    mine = owner(me)

    def signal(sem, section, column=None):
        pl.semaphore_signal(
            sem, inc=1, device_id=(section, tp if column is None else column), device_id_type=MESH
        )

    barrier = pltpu.get_barrier_semaphore()
    for px, py in ((1, 0), (-1, 0), (0, 1), (0, -1)):
        signal(barrier, ctx, at(x + px, y_at + py))
    signal(barrier, ctx + 1 - 2 * core)

    @pl.when(z < 7)
    def _():
        signal(barrier, ctx + 2)

    @pl.when(group == 0)
    def _():
        signal(barrier, mirror)

    weights = [
        pltpu.make_async_copy(a, b, w_sem.at[i])
        for i, (a, b) in enumerate(((wx, vx), (wbc, vbc), (wz, vz)))
    ]
    own = pltpu.make_async_copy(tok, held.at[tp], own_sem)
    own.start()
    for w in weights:
        w.start()
    pl.semaphore_wait(barrier, 5 + lax.min(z, 1) + group)

    def slot(dx, dy):
        return at(x - dx, y_at - dy)

    def piece(s, half):
        return held.at[s, pl.ds(half * HALF, HALF), :]

    def dxy(half, first, second):
        return (second, first) if half == 0 else (first, second)

    def send(half, source, direction, along, landing):
        dx, dy = dxy(half, *source)
        px, py = dxy(half, *((direction, 0) if along == 0 else (0, direction)))
        first, second = landing
        s = slot(dx, dy)
        src = tok.at[pl.ds(half * HALF, HALF), :] if all(isinstance(v, int) and v == 0 for v in source) else piece(s, half)
        pltpu.make_async_remote_copy(
            src_ref=src,
            dst_ref=piece(s, half),
            send_sem=g_send,
            recv_sem=g_recv.at[half, first * SIDE + second],
            device_id=(ctx, at(x + px, y_at + py)),
            device_id_type=MESH,
        ).start()

    def arrived(half, first, second):
        p = piece(slot(*dxy(half, first, second)), half)
        pltpu.make_async_copy(p, p, g_recv.at[half, first * SIDE + second]).wait()

    def along_second(half, first):
        send(half, (first, 0), 1, 1, (first, 1))
        send(half, (first, 0), -1, 1, (first, 3))

    def across_second(half, first):
        flag = lax.rem(first + core, 2)
        send(half, (first, 1 + 2 * flag), 1 - 2 * flag, 1, (first, 2))

    def multiply(dx, dy, begin=False):
        s = slot(dx, dy)
        a = held[s]
        depth = pl.ds(pl.multiple_of(s * FEAT, FEAT), FEAT)
        for acc, v in ((acc_x, vx), (acc_bc, vbc), (acc_z, vz)):
            part = dot(a, v[depth, :])
            acc[...] = part if begin else acc[...] + part

    def multiply_all(count, offsets):
        def body(i, c):
            multiply(*offsets(i))
            return c

        lax.fori_loop(0, count, body, 0)

    for half in (0, 1):
        send(half, (0, 0), 1, 0, (1, 0))
        send(half, (0, 0), -1, 0, (3, 0))
    for half in (0, 1):
        along_second(half, 0)

    @pl.when(group == 1)
    def _():
        signal(facing, mirror)

    @pl.when(place == 3)
    def _():
        signal(up, ctx - 2)

    def sweep_up(at_place):
        @pl.when(place == at_place)
        def _():
            pl.semaphore_wait(up, 1)
            if at_place == 0:
                signal(down, ctx + 2)

        @pl.when(jnp.logical_and(place == at_place, z > 0))
        def _():
            signal(up, ctx - 2)

    def sweep_down(at_place):
        @pl.when(place == at_place)
        def _():
            pl.semaphore_wait(down, 1)
            if at_place < 3:
                signal(down, ctx + 2)

    i0 = lax.broadcasted_iota(jnp.int32, (ROWS, ROWS), 0)
    i1 = lax.broadcasted_iota(jnp.int32, (ROWS, ROWS), 1)
    upper = (i0 <= i1).astype(F32)
    cum_t = dot(decay_t[...], upper, precision=lax.Precision.HIGHEST)
    lane = lax.broadcasted_iota(jnp.int32, (1, 128), 1)
    for t in range(LT):
        rows = jnp.concatenate(
            [jnp.broadcast_to(cum_t[2 * t + k : 2 * t + k + 1], (64, ROWS)) for k in (0, 1)], 0
        )
        cum = rows.T
        total = cum[ROWS - 1 : ROWS]
        step_row = jnp.where(lane < 64, step[2 * t], step[2 * t + 1])
        grow[t] = jnp.exp(cum)
        end_w[t] = jnp.exp(total - cum) * step_row
        tot_out[t] = jnp.broadcast_to(jnp.exp(total), (8, 128))

    for half in (0, 1):
        arrived(half, 1, 0)
        arrived(half, 3, 0)
        send(half, (1 + 2 * core, 0), 1 - 2 * core, 0, (2, 0))
        along_second(half, 1)
        along_second(half, 3)
    for h in range(8):
        if h == 4:
            for half in (0, 1):
                arrived(half, 0, 1)
                arrived(half, 0, 3)
                across_second(half, 0)
        row = cum_t[h : h + 1]
        col = jnp.broadcast_to(row, (128, ROWS)).T
        col = jnp.concatenate([col, col], axis=1)
        keep = i0 >= i1
        seg[h] = jnp.where(keep, jnp.exp(jnp.where(keep, col - row, 0.0)), 0.0) * step[h]

    own.wait()
    for w in weights:
        w.wait()
    multiply(0, 0, True)
    for half in (0, 1):
        arrived(half, 2, 0)
        along_second(half, 2)

    def beside(i):
        o, swap = 1 + 2 * lax.rem(i, 2), lax.div(i, 2)
        return swap * o, (1 - swap) * o

    multiply_all(4, beside)
    for half in (0, 1):
        arrived(half, 1, 1)
        arrived(half, 1, 3)
        across_second(half, 1)
    sweep_up(2)
    for half in (0, 1):
        arrived(half, 3, 1)
        arrived(half, 3, 3)
        across_second(half, 3)
    sweep_up(1)
    multiply_all(4, lambda i: (1 + 2 * lax.rem(i, 2), 1 + 2 * lax.div(i, 2)))
    for half in (0, 1):
        arrived(half, 0, 2)
    sweep_up(0)
    multiply_all(2, lambda i: (2 * (1 - i), 2 * i))
    for half in (0, 1):
        arrived(half, 2, 1)
        arrived(half, 2, 3)
        across_second(half, 2)
    sweep_down(1)
    for half in (0, 1):
        arrived(half, 1, 2)
        arrived(half, 3, 2)

    def far(i):
        o, swap = 1 + 2 * lax.rem(i, 2), lax.div(i, 2)
        return o + swap * (2 - o), 2 + swap * (o - 2)

    multiply_all(4, far)
    sweep_down(2)
    for half in (0, 1):
        arrived(half, 2, 2)
    multiply(2, 2)
    sweep_down(3)

    for t in range(LT + 1):
        p = acc_bc[...] if t == LT else acc_x[:, t * 128 : (t + 1) * 128]
        p = p.astype(BF16)
        rim_out[t] = p[ROWS - 16 :]
        pre[t, 8 : 8 + ROWS] = p.astype(F32)
    rim = pltpu.make_async_remote_copy(
        src_ref=rim_out,
        dst_ref=rim_in,
        send_sem=rim_sem.at[0],
        recv_sem=rim_sem.at[1],
        device_id=(lax.min(ctx + 1, SECTIONS - 1), tp),
        device_id_type=MESH,
    )

    @pl.when(z == 3)
    def _():
        pl.semaphore_wait(up, 1)

    @pl.when(ctx < SECTIONS - 1)
    def _():
        rim.start()

    tot_in[me] = tot_out[lax.div(mine, 2)]

    def send_total(i, c):
        q = lax.rem(me + i, PEERS)
        pltpu.make_async_remote_copy(
            src_ref=tot_out.at[lax.div(owner(q), 2)],
            dst_ref=tot_in.at[me],
            send_sem=tot_send,
            recv_sem=tot_recv,
            device_id=(group * PEERS + q, tp),
            device_id_type=MESH,
        ).start()
        return c

    lax.fori_loop(1, PEERS, send_total, 0)

    @pl.when(ctx == 0)
    def _():
        rim_in[...] = jnp.zeros_like(rim_in)

    @pl.when(ctx > 0)
    def _():
        rim.wait_recv()

    def conv(t):
        pre[t, 0:8] = rim_in[t].astype(F32)[8:]
        cols = slice(0, 128) if t == LT else slice(t * 128, (t + 1) * 128)
        taps, bias = (conv_bc, bias_bc) if t == LT else (conv_x, bias_x)
        total = bias[:, cols] + jnp.zeros((ROWS, 128), F32)
        for k in range(TAPS):
            total = total + taps[k : k + 1, cols] * pre[t, 5 + k : 5 + k + ROWS]
        return silu(total).astype(BF16)

    side = lax.rem(tp, 2)
    bc[side] = conv(LT)
    swap = pltpu.make_async_remote_copy(
        src_ref=bc.at[side],
        dst_ref=bc.at[side],
        send_sem=bc_sem.at[0],
        recv_sem=bc_sem.at[1],
        device_id=(ctx, mate),
        device_id_type=MESH,
    )
    swap.start()
    for t in range(LT):
        xs[t] = conv(t)
    other = bc.at[1 - side]
    pltpu.make_async_copy(other, other, bc_sem.at[1]).wait()

    b_t = bc[0].astype(F32).T.astype(BF16)
    for t in range(LT):
        weighted = (xs[t].astype(F32) * end_w[t]).astype(BF16)
        st_out[2 * t : 2 * t + 2] = dot(b_t, weighted).reshape(2, SLICE, 128).astype(BF16)
    st_in[me] = st_out[mine]

    def send_state(i, c):
        q = lax.rem(me + i, PEERS)
        pltpu.make_async_remote_copy(
            src_ref=st_out.at[owner(q)],
            dst_ref=st_in.at[me],
            send_sem=st_send,
            recv_sem=st_recv.at[me],
            device_id=(group * PEERS + q, tp),
            device_id_type=MESH,
        ).start()
        return c

    lax.fori_loop(1, PEERS, send_state, 0)

    scores = dot(bc[1], b_t)

    def intra(t):
        both = [dot((seg[2 * t + k] * scores).astype(BF16), xs[t]) for k in (0, 1)]
        skip_row = jnp.where(lane < 64, skip[2 * t], skip[2 * t + 1])
        y[t] = jnp.where(lane < 64, both[0], both[1]) + skip_row * xs[t].astype(F32)

    for t in range(LT):
        intra(t)
    for t in range(LT):
        g = acc_z[:, t * 128 : (t + 1) * 128].astype(BF16).astype(F32)
        acc_z[:, t * 128 : (t + 1) * 128] = silu(g)

    def all_but_one(ref, sem):
        part = ref.at[pl.ds(0, ref.shape[0] - 1)]
        pltpu.make_async_copy(part, part, sem).wait()

    all_but_one(tot_in, tot_recv)
    total_of_half = pltpu.make_async_remote_copy(
        src_ref=half_out,
        dst_ref=half_in,
        send_sem=half_sem.at[0],
        recv_sem=half_sem.at[1],
        device_id=(lax.max(mirror, PEERS), tp),
        device_id_type=MESH,
    )

    @pl.when(group == 0)
    def _():
        half_in[...] = jnp.zeros_like(half_in)

    @pl.when(group == 1)
    def _():
        total_of_half.wait_recv()

    def entering_copy(q):
        return pltpu.make_async_remote_copy(
            src_ref=en_out.at[q],
            dst_ref=en_in.at[mine],
            send_sem=en_send.at[q],
            recv_sem=en_recv,
            device_id=(group * PEERS + q, tp),
            device_id_type=MESH,
        )

    def sends(q):
        return jnp.logical_and(me != q, group * PEERS + q > 0)

    state = half_in[...].astype(F32)
    for q in range(PEERS):
        en_out[q] = state.astype(BF16)

        @pl.when(sends(q))
        def _(q=q):
            entering_copy(q).start()

        @pl.when(me != q)
        def _(q=q):
            pltpu.make_async_copy(st_in.at[q], st_in.at[q], st_recv.at[q]).wait()

        state = tot_in[q][0:1] * state + st_in[q].astype(F32)
    half_out[...] = state.astype(BF16)

    @pl.when(group == 0)
    def _():
        pl.semaphore_wait(facing, 1)
        total_of_half.start()

    en_in[mine] = en_out[me]

    @pl.when(ctx == 0)
    def _():
        en_in[...] = jnp.zeros_like(en_in)

    @pl.when(ctx > 0)
    def _():
        all_but_one(en_in, en_recv)

    squares = jnp.zeros((ROWS, 128), F32)
    for t in range(LT):
        entering = en_in[2 * t : 2 * t + 2].reshape(128, 128)
        gated = (y[t] + grow[t] * dot(bc[1], entering)) * acc_z[:, t * 128 : (t + 1) * 128]
        squares = squares + gated * gated
        y[t] = gated
    local = jnp.sum(squares.T, axis=0, keepdims=True)
    sq_out[...] = jnp.broadcast_to(local, (8, ROWS))
    norm = pltpu.make_async_remote_copy(
        src_ref=sq_out,
        dst_ref=sq_in,
        send_sem=sq_sem.at[0],
        recv_sem=sq_sem.at[1],
        device_id=(ctx, mate),
        device_id_type=MESH,
    )
    norm.start()
    norm.wait_recv()
    mean = (sq_out[0:1] + sq_in[0:1]) * (1.0 / (2 * LT * 128))
    scale = jnp.broadcast_to(lax.rsqrt(mean + 1e-5), (128, ROWS)).T
    for t in range(LT):
        cols = slice(t * 128, (t + 1) * 128)
        out[:, cols] = (y[t] * scale * gain[:, cols]).astype(BF16)

    norm.wait_send()
    swap.wait_send()
    all_but_one(held, g_send)
    all_but_one(tot_in, tot_send)
    all_but_one(st_out, st_send)

    @pl.when(ctx < SECTIONS - 1)
    def _():
        rim.wait_send()

    @pl.when(group == 0)
    def _():
        total_of_half.wait_send()

    for q in range(PEERS):

        @pl.when(sends(q))
        def _(q=q):
            entering_copy(q).wait_send()


def local(tokens, w_z, w_x, w_bc, conv_x, conv_bc, bias_x, bias_bc, decay, step, skip, gain):
    hbm = pl.BlockSpec(memory_space=pl.ANY)
    vmem = pl.BlockSpec(memory_space=pltpu.VMEM)
    smem = pl.BlockSpec(memory_space=pltpu.SMEM)
    width = w_x.shape[1]
    dma = pltpu.SemaphoreType.DMA
    scratch = [
        pltpu.VMEM((16, ROWS, FEAT), BF16),
        pltpu.VMEM(w_z.shape, BF16),
        pltpu.VMEM(w_x.shape, BF16),
        pltpu.VMEM(w_bc.shape, BF16),
        pltpu.VMEM((ROWS, width), F32),
        pltpu.VMEM((ROWS, width), F32),
        pltpu.VMEM((ROWS, 128), F32),
        pltpu.VMEM((LT + 1, 8 + ROWS, 128), F32),
        pltpu.VMEM((LT + 1, 16, 128), BF16),
        pltpu.VMEM((LT + 1, 16, 128), BF16),
        pltpu.VMEM((LT, ROWS, 128), BF16),
        pltpu.VMEM((2, ROWS, 128), BF16),
        pltpu.VMEM((8, ROWS, ROWS), F32),
        pltpu.VMEM((LT, ROWS, 128), F32),
        pltpu.VMEM((LT, ROWS, 128), F32),
        pltpu.VMEM((LT, 8, 128), F32),
        pltpu.VMEM((PEERS, 8, 128), F32),
        pltpu.VMEM((PEERS, SLICE, 128), BF16),
        pltpu.VMEM((PEERS, SLICE, 128), BF16),
        pltpu.VMEM((PEERS, SLICE, 128), BF16),
        pltpu.VMEM((PEERS, SLICE, 128), BF16),
        pltpu.VMEM((SLICE, 128), BF16),
        pltpu.VMEM((SLICE, 128), BF16),
        pltpu.VMEM((LT, ROWS, 128), F32),
        pltpu.VMEM((8, ROWS), F32),
        pltpu.VMEM((8, ROWS), F32),
        dma((3,)),
        dma,
        dma,
        dma((2, 16)),
        dma,
        dma,
        dma((2,)),
        dma((2,)),
        dma,
        dma((PEERS,)),
        dma((PEERS,)),
        dma,
        dma((2,)),
        dma((2,)),
        pltpu.SemaphoreType.REGULAR,
        pltpu.SemaphoreType.REGULAR,
        pltpu.SemaphoreType.REGULAR,
    ]
    return pl.pallas_call(
        kernel,
        out_shape=jax.ShapeDtypeStruct((ROWS, width), BF16),
        in_specs=[hbm] * 4 + [vmem] * 5 + [smem] * 2 + [vmem],
        out_specs=vmem,
        scratch_shapes=scratch,
        compiler_params=pltpu.CompilerParams(
            collective_id=0, has_side_effects=True, vmem_limit_bytes=56 * 2**20
        ),
    )(
        tokens, w_z, w_x, w_bc, conv_x, conv_bc, bias_x.reshape(1, -1), bias_bc.reshape(1, -1),
        decay.T, step, skip, gain.reshape(1, -1),
    )


def solution(mesh):
    return jax.shard_map(
        local,
        mesh=mesh,
        in_specs=(
            P("ctx", "tp"),
            P(None, "tp"),
            P(None, "tp"),
            P(None, "tp"),
            P(None, "tp"),
            P(None, "tp"),
            P("tp"),
            P("tp"),
            P("ctx", "tp"),
            P("tp"),
            P("tp"),
            P("tp"),
        ),
        out_specs=P("ctx", "tp"),
        check_vma=False,
    )
```

```python
import jax
import jax.numpy as jnp
from jax import lax
from jax.experimental import pallas as pl
from jax.experimental.pallas import tpu as pltpu
from jax.sharding import PartitionSpec as P

MESH = pl.DeviceIdType.MESH
SIDE = 4
TAPS = 4
ROWS = 256
HALF = 128
FEAT = 256
SECTIONS = 16
PEERS = 8
SLICE = 64
LT = 4
F32 = jnp.float32
BF16 = jnp.bfloat16


def silu(v):
    return v / (1.0 + jnp.exp(-v))


def dot(a, b, **kw):
    return jnp.dot(a, b, preferred_element_type=F32, **kw)


def kernel(
    tok, wz, wx, wbc, conv_x, conv_bc, bias_x, bias_bc, decay_t, step, skip, gain, out,
    held, vz, vx, vbc, acc_z, acc_x, acc_bc, pre, rim_out, rim_in, xs, bc, seg, grow, end_w,
    tot_out, tot_in, st_out, st_in, en_out, en_in, half_out, half_in, y, sq_out, sq_in,
    w_sem, own_sem, g_send, g_recv, tot_send, tot_recv, rim_sem, bc_sem, st_send, st_recv,
    en_send, en_recv, half_sem, sq_sem, up, down, facing,
):
    ctx, tp = lax.axis_index("ctx"), lax.axis_index("tp")
    core = lax.rem(ctx, 2)
    x, y_at = lax.div(tp, SIDE), lax.rem(tp, SIDE)

    def at(px, py):
        return lax.rem(px + 2 * SIDE, SIDE) * SIDE + lax.rem(py + 2 * SIDE, SIDE)

    mate = at(x, y_at + 1 - 2 * lax.rem(y_at, 2))
    z = lax.div(ctx, 2)
    group, me = lax.div(ctx, PEERS), lax.rem(ctx, PEERS)
    place = lax.rem(z, 4)
    far_place = lax.rem(place + 2, 4)
    facing_at = ((1 - group) * 4 + far_place) * 2 + core

    def owner(o):
        p = lax.rem(lax.div(o, 2) + 2 * group, 4)
        return p * 2 + lax.rem(o, 2)

    mine = owner(me)

    def signal(sem, section, column=None):
        pl.semaphore_signal(
            sem, inc=1, device_id=(section, tp if column is None else column), device_id_type=MESH
        )

    barrier = pltpu.get_barrier_semaphore()
    for px, py in ((1, 0), (-1, 0), (0, 1), (0, -1), (2, 0), (0, 2)):
        signal(barrier, ctx, at(x + px, y_at + py))
    signal(barrier, ctx + 1 - 2 * core)

    @pl.when(z < 7)
    def _():
        signal(barrier, ctx + 2)

    @pl.when(group == 0)
    def _():
        signal(barrier, facing_at)

    weights = [
        pltpu.make_async_copy(a, b, w_sem.at[i])
        for i, (a, b) in enumerate(((wx, vx), (wbc, vbc), (wz, vz)))
    ]
    own = pltpu.make_async_copy(tok, held.at[tp], own_sem)
    own.start()
    for w in weights:
        w.start()
    pl.semaphore_wait(barrier, 7 + lax.min(z, 1) + group)

    def slot(dx, dy):
        return at(x - dx, y_at - dy)

    def piece(s, half):
        return held.at[s, pl.ds(half * HALF, HALF), :]

    def dxy(half, first, second):
        return (second, first) if half == 0 else (first, second)

    def send(half, source, direction, along, landing):
        dx, dy = dxy(half, *source)
        px, py = dxy(half, *((direction, 0) if along == 0 else (0, direction)))
        first, second = landing
        s = slot(dx, dy)
        src = tok.at[pl.ds(half * HALF, HALF), :] if all(isinstance(v, int) and v == 0 for v in source) else piece(s, half)
        pltpu.make_async_remote_copy(
            src_ref=src,
            dst_ref=piece(s, half),
            send_sem=g_send,
            recv_sem=g_recv.at[half, first * SIDE + second],
            device_id=(ctx, at(x + px, y_at + py)),
            device_id_type=MESH,
        ).start()

    def arrived(half, first, second):
        p = piece(slot(*dxy(half, first, second)), half)
        pltpu.make_async_copy(p, p, g_recv.at[half, first * SIDE + second]).wait()

    def along_second(half, first):
        if first == 3:

            @pl.when(core == 0)
            def _():
                send(half, (first, 0), 2, 1, (first, 2))

        send(half, (first, 0), 1, 1, (first, 1))
        send(half, (first, 0), -1, 1, (first, 3))

    def across_second(half, first):
        flag = lax.rem(first + core, 2)

        @pl.when(jnp.logical_or(core == 1, first < 3))
        def _():
            send(half, (first, 1 + 2 * flag), 1 - 2 * flag, 1, (first, 2))

    def multiply(dx, dy, begin=False):
        s = slot(dx, dy)
        a = held[s]
        depth = pl.ds(pl.multiple_of(s * FEAT, FEAT), FEAT)
        for acc, v in ((acc_x, vx), (acc_bc, vbc), (acc_z, vz)):
            part = dot(a, v[depth, :])
            acc[...] = part if begin else acc[...] + part

    def multiply_all(count, offsets):
        def body(i, c):
            multiply(*offsets(i))
            return c

        lax.fori_loop(0, count, body, 0)

    for half in (0, 1):
        send(half, (0, 0), 2, 0, (2, 0))
    for half in (0, 1):
        send(half, (0, 0), 1, 0, (1, 0))
        send(half, (0, 0), -1, 0, (3, 0))
    for half in (0, 1):
        along_second(half, 0)

    @pl.when(group == 1)
    def _():
        signal(facing, facing_at)

    @pl.when(place == 3)
    def _():
        signal(up, ctx - 2)

    def sweep_up(at_place):
        @pl.when(place == at_place)
        def _():
            pl.semaphore_wait(up, 1)
            if at_place == 0:
                signal(down, ctx + 2)

        @pl.when(jnp.logical_and(place == at_place, z > 0))
        def _():
            signal(up, ctx - 2)

    def sweep_down(at_place):
        @pl.when(place == at_place)
        def _():
            pl.semaphore_wait(down, 1)
            if at_place < 3:
                signal(down, ctx + 2)

    i0 = lax.broadcasted_iota(jnp.int32, (ROWS, ROWS), 0)
    i1 = lax.broadcasted_iota(jnp.int32, (ROWS, ROWS), 1)
    upper = (i0 <= i1).astype(F32)
    cum_t = dot(decay_t[...], upper, precision=lax.Precision.HIGHEST)
    lane = lax.broadcasted_iota(jnp.int32, (1, 128), 1)
    for t in range(LT):
        rows = jnp.concatenate(
            [jnp.broadcast_to(cum_t[2 * t + k : 2 * t + k + 1], (64, ROWS)) for k in (0, 1)], 0
        )
        cum = rows.T
        total = cum[ROWS - 1 : ROWS]
        step_row = jnp.where(lane < 64, step[2 * t], step[2 * t + 1])
        grow[t] = jnp.exp(cum)
        end_w[t] = jnp.exp(total - cum) * step_row
        tot_out[t] = jnp.broadcast_to(jnp.exp(total), (8, 128))

    for half in (0, 1):
        arrived(half, 2, 0)
        along_second(half, 2)
    for half in (0, 1):
        arrived(half, 1, 0)
        along_second(half, 1)
        arrived(half, 3, 0)
        along_second(half, 3)
    for h in range(8):
        if h == 4:
            for half in (0, 1):
                arrived(half, 0, 1)
                arrived(half, 0, 3)
                across_second(half, 0)
        row = cum_t[h : h + 1]
        col = jnp.broadcast_to(row, (128, ROWS)).T
        col = jnp.concatenate([col, col], axis=1)
        keep = i0 >= i1
        seg[h] = jnp.where(keep, jnp.exp(jnp.where(keep, col - row, 0.0)), 0.0) * step[h]

    for half in (0, 1):
        arrived(half, 2, 1)
        arrived(half, 2, 3)
        across_second(half, 2)
    own.wait()
    for w in weights:
        w.wait()
    multiply(0, 0, True)

    def beside(i):
        o, swap = 1 + 2 * lax.rem(i, 2), lax.div(i, 2)
        return swap * o, (1 - swap) * o

    multiply_all(4, beside)
    sweep_up(2)
    for half in (0, 1):
        arrived(half, 1, 1)
        arrived(half, 1, 3)
        across_second(half, 1)
    for half in (0, 1):
        arrived(half, 3, 1)
        arrived(half, 3, 3)
        across_second(half, 3)
    sweep_up(1)
    multiply_all(4, lambda i: (1 + 2 * lax.rem(i, 2), 1 + 2 * lax.div(i, 2)))
    sweep_up(0)
    for half in (0, 1):
        arrived(half, 0, 2)
    multiply_all(2, lambda i: (2 * (1 - i), 2 * i))
    sweep_down(1)
    for half in (0, 1):
        arrived(half, 1, 2)
        arrived(half, 3, 2)

    def far(i):
        o, swap = 1 + 2 * lax.rem(i, 2), lax.div(i, 2)
        return o + swap * (2 - o), 2 + swap * (o - 2)

    multiply_all(4, far)
    sweep_down(2)
    for half in (0, 1):
        arrived(half, 2, 2)
    multiply(2, 2)
    sweep_down(3)

    for t in range(LT + 1):
        p = acc_bc[...] if t == LT else acc_x[:, t * 128 : (t + 1) * 128]
        p = p.astype(BF16)
        rim_out[t] = p[ROWS - 16 :]
        pre[t, 8 : 8 + ROWS] = p.astype(F32)
    rim = pltpu.make_async_remote_copy(
        src_ref=rim_out,
        dst_ref=rim_in,
        send_sem=rim_sem.at[0],
        recv_sem=rim_sem.at[1],
        device_id=(lax.min(ctx + 1, SECTIONS - 1), tp),
        device_id_type=MESH,
    )

    @pl.when(z == 3)
    def _():
        pl.semaphore_wait(up, 1)

    @pl.when(ctx < SECTIONS - 1)
    def _():
        rim.start()

    tot_in[me] = tot_out[lax.div(mine, 2)]

    def send_total(i, c):
        q = lax.rem(me + i, PEERS)
        pltpu.make_async_remote_copy(
            src_ref=tot_out.at[lax.div(owner(q), 2)],
            dst_ref=tot_in.at[me],
            send_sem=tot_send,
            recv_sem=tot_recv,
            device_id=(group * PEERS + q, tp),
            device_id_type=MESH,
        ).start()
        return c

    lax.fori_loop(1, PEERS, send_total, 0)

    @pl.when(ctx == 0)
    def _():
        rim_in[...] = jnp.zeros_like(rim_in)

    @pl.when(ctx > 0)
    def _():
        rim.wait_recv()

    def conv(t):
        pre[t, 0:8] = rim_in[t].astype(F32)[8:]
        cols = slice(0, 128) if t == LT else slice(t * 128, (t + 1) * 128)
        taps, bias = (conv_bc, bias_bc) if t == LT else (conv_x, bias_x)
        total = bias[:, cols] + jnp.zeros((ROWS, 128), F32)
        for k in range(TAPS):
            total = total + taps[k : k + 1, cols] * pre[t, 5 + k : 5 + k + ROWS]
        return silu(total).astype(BF16)

    side = lax.rem(tp, 2)
    bc[side] = conv(LT)
    swap = pltpu.make_async_remote_copy(
        src_ref=bc.at[side],
        dst_ref=bc.at[side],
        send_sem=bc_sem.at[0],
        recv_sem=bc_sem.at[1],
        device_id=(ctx, mate),
        device_id_type=MESH,
    )
    swap.start()
    for t in range(LT):
        xs[t] = conv(t)
    other = bc.at[1 - side]
    pltpu.make_async_copy(other, other, bc_sem.at[1]).wait()

    b_t = bc[0].astype(F32).T.astype(BF16)
    for t in range(LT):
        weighted = (xs[t].astype(F32) * end_w[t]).astype(BF16)
        st_out[2 * t : 2 * t + 2] = dot(b_t, weighted).reshape(2, SLICE, 128).astype(BF16)
    st_in[me] = st_out[mine]

    def send_state(i, c):
        q = lax.rem(me + i, PEERS)
        pltpu.make_async_remote_copy(
            src_ref=st_out.at[owner(q)],
            dst_ref=st_in.at[me],
            send_sem=st_send,
            recv_sem=st_recv.at[me],
            device_id=(group * PEERS + q, tp),
            device_id_type=MESH,
        ).start()
        return c

    lax.fori_loop(1, PEERS, send_state, 0)

    scores = dot(bc[1], b_t)

    def intra(t):
        both = [dot((seg[2 * t + k] * scores).astype(BF16), xs[t]) for k in (0, 1)]
        skip_row = jnp.where(lane < 64, skip[2 * t], skip[2 * t + 1])
        y[t] = jnp.where(lane < 64, both[0], both[1]) + skip_row * xs[t].astype(F32)

    for t in range(LT):
        intra(t)
    for t in range(LT):
        g = acc_z[:, t * 128 : (t + 1) * 128].astype(BF16).astype(F32)
        acc_z[:, t * 128 : (t + 1) * 128] = silu(g)

    def all_but_one(ref, sem):
        part = ref.at[pl.ds(0, ref.shape[0] - 1)]
        pltpu.make_async_copy(part, part, sem).wait()

    all_but_one(tot_in, tot_recv)
    total_of_half = pltpu.make_async_remote_copy(
        src_ref=half_out,
        dst_ref=half_in,
        send_sem=half_sem.at[0],
        recv_sem=half_sem.at[1],
        device_id=(lax.max(facing_at, PEERS), tp),
        device_id_type=MESH,
    )

    @pl.when(group == 0)
    def _():
        half_in[...] = jnp.zeros_like(half_in)

    @pl.when(group == 1)
    def _():
        total_of_half.wait_recv()

    def entering_copy(q):
        return pltpu.make_async_remote_copy(
            src_ref=en_out.at[q],
            dst_ref=en_in.at[mine],
            send_sem=en_send.at[q],
            recv_sem=en_recv,
            device_id=(group * PEERS + q, tp),
            device_id_type=MESH,
        )

    def sends(q):
        return jnp.logical_and(me != q, group * PEERS + q > 0)

    state = half_in[...].astype(F32)
    for q in range(PEERS):
        en_out[q] = state.astype(BF16)

        @pl.when(sends(q))
        def _(q=q):
            entering_copy(q).start()

        @pl.when(me != q)
        def _(q=q):
            pltpu.make_async_copy(st_in.at[q], st_in.at[q], st_recv.at[q]).wait()

        state = tot_in[q][0:1] * state + st_in[q].astype(F32)
    half_out[...] = state.astype(BF16)

    @pl.when(group == 0)
    def _():
        pl.semaphore_wait(facing, 1)
        total_of_half.start()

    en_in[mine] = en_out[me]

    @pl.when(ctx == 0)
    def _():
        en_in[...] = jnp.zeros_like(en_in)

    @pl.when(ctx > 0)
    def _():
        all_but_one(en_in, en_recv)

    squares = jnp.zeros((ROWS, 128), F32)
    for t in range(LT):
        entering = en_in[2 * t : 2 * t + 2].reshape(128, 128)
        gated = (y[t] + grow[t] * dot(bc[1], entering)) * acc_z[:, t * 128 : (t + 1) * 128]
        squares = squares + gated * gated
        y[t] = gated
    local = jnp.sum(squares.T, axis=0, keepdims=True)
    sq_out[...] = jnp.broadcast_to(local, (8, ROWS))
    norm = pltpu.make_async_remote_copy(
        src_ref=sq_out,
        dst_ref=sq_in,
        send_sem=sq_sem.at[0],
        recv_sem=sq_sem.at[1],
        device_id=(ctx, mate),
        device_id_type=MESH,
    )
    norm.start()
    norm.wait_recv()
    mean = (sq_out[0:1] + sq_in[0:1]) * (1.0 / (2 * LT * 128))
    scale = jnp.broadcast_to(lax.rsqrt(mean + 1e-5), (128, ROWS)).T
    for t in range(LT):
        cols = slice(t * 128, (t + 1) * 128)
        out[:, cols] = (y[t] * scale * gain[:, cols]).astype(BF16)

    norm.wait_send()
    swap.wait_send()
    all_but_one(held, g_send)
    all_but_one(tot_in, tot_send)
    all_but_one(st_out, st_send)

    @pl.when(ctx < SECTIONS - 1)
    def _():
        rim.wait_send()

    @pl.when(group == 0)
    def _():
        total_of_half.wait_send()

    for q in range(PEERS):

        @pl.when(sends(q))
        def _(q=q):
            entering_copy(q).wait_send()


def local(tokens, w_z, w_x, w_bc, conv_x, conv_bc, bias_x, bias_bc, decay, step, skip, gain):
    hbm = pl.BlockSpec(memory_space=pl.ANY)
    vmem = pl.BlockSpec(memory_space=pltpu.VMEM)
    smem = pl.BlockSpec(memory_space=pltpu.SMEM)
    width = w_x.shape[1]
    dma = pltpu.SemaphoreType.DMA
    scratch = [
        pltpu.VMEM((16, ROWS, FEAT), BF16),
        pltpu.VMEM(w_z.shape, BF16),
        pltpu.VMEM(w_x.shape, BF16),
        pltpu.VMEM(w_bc.shape, BF16),
        pltpu.VMEM((ROWS, width), F32),
        pltpu.VMEM((ROWS, width), F32),
        pltpu.VMEM((ROWS, 128), F32),
        pltpu.VMEM((LT + 1, 8 + ROWS, 128), F32),
        pltpu.VMEM((LT + 1, 16, 128), BF16),
        pltpu.VMEM((LT + 1, 16, 128), BF16),
        pltpu.VMEM((LT, ROWS, 128), BF16),
        pltpu.VMEM((2, ROWS, 128), BF16),
        pltpu.VMEM((8, ROWS, ROWS), F32),
        pltpu.VMEM((LT, ROWS, 128), F32),
        pltpu.VMEM((LT, ROWS, 128), F32),
        pltpu.VMEM((LT, 8, 128), F32),
        pltpu.VMEM((PEERS, 8, 128), F32),
        pltpu.VMEM((PEERS, SLICE, 128), BF16),
        pltpu.VMEM((PEERS, SLICE, 128), BF16),
        pltpu.VMEM((PEERS, SLICE, 128), BF16),
        pltpu.VMEM((PEERS, SLICE, 128), BF16),
        pltpu.VMEM((SLICE, 128), BF16),
        pltpu.VMEM((SLICE, 128), BF16),
        pltpu.VMEM((LT, ROWS, 128), F32),
        pltpu.VMEM((8, ROWS), F32),
        pltpu.VMEM((8, ROWS), F32),
        dma((3,)),
        dma,
        dma,
        dma((2, 16)),
        dma,
        dma,
        dma((2,)),
        dma((2,)),
        dma,
        dma((PEERS,)),
        dma((PEERS,)),
        dma,
        dma((2,)),
        dma((2,)),
        pltpu.SemaphoreType.REGULAR,
        pltpu.SemaphoreType.REGULAR,
        pltpu.SemaphoreType.REGULAR,
    ]
    return pl.pallas_call(
        kernel,
        out_shape=pltpu.VMEM((ROWS, width), BF16),
        in_specs=[hbm] * 4 + [vmem] * 5 + [smem] * 2 + [vmem],
        out_specs=vmem,
        scratch_shapes=scratch,
        compiler_params=pltpu.CompilerParams(
            collective_id=0, has_side_effects=True, vmem_limit_bytes=56 * 2**20
        ),
    )(
        tokens, w_z, w_x, w_bc, conv_x, conv_bc, bias_x.reshape(1, -1), bias_bc.reshape(1, -1),
        decay.T, step, skip, gain.reshape(1, -1),
    )


def solution(mesh):
    return jax.shard_map(
        local,
        mesh=mesh,
        in_specs=(
            P("ctx", "tp"),
            P(None, "tp"),
            P(None, "tp"),
            P(None, "tp"),
            P(None, "tp"),
            P(None, "tp"),
            P("tp"),
            P("tp"),
            P("ctx", "tp"),
            P("tp"),
            P("tp"),
            P("tp"),
        ),
        out_specs=P("ctx", "tp"),
        check_vma=False,
    )
```

```python
import jax
import jax.numpy as jnp
from jax import lax
from jax.experimental import pallas as pl
from jax.experimental.pallas import tpu as pltpu
from jax.sharding import PartitionSpec as P

MESH = pl.DeviceIdType.MESH
SIDE = 4
TAPS = 4
ROWS = 256
HALF = 128
FEAT = 256
SECTIONS = 16
PEERS = 8
LT = 4
F32 = jnp.float32
BF16 = jnp.bfloat16


def silu(v):
    return v / (1.0 + jnp.exp(-v))


def dot(a, b, **kw):
    return jnp.dot(a, b, preferred_element_type=F32, **kw)


def kernel(
    tok, wz, wx, wbc, conv_x, conv_bc, bias_x, bias_bc, decay_t, step, skip, gain, out,
    held, vz, vx, vbc, acc_z, acc_x, acc_bc, pre, rim_out, rim_in, xs, bc, seg, grow, end_w,
    tot_out, tot_in, st_out, st_in, en_out, en_in, half_out, half_in, within, remains, y, sq_out, sq_in,
    w_sem, own_sem, g_send, g_recv, tot_send, tot_recv, rim_sem, bc_sem, st_send, st_recv,
    en_send, en_recv, half_sem, sq_sem, up, down, facing,
):
    ctx, tp = lax.axis_index("ctx"), lax.axis_index("tp")
    core = lax.rem(ctx, 2)
    x, y_at = lax.div(tp, SIDE), lax.rem(tp, SIDE)

    def at(px, py):
        return lax.rem(px + 2 * SIDE, SIDE) * SIDE + lax.rem(py + 2 * SIDE, SIDE)

    mate = at(x, y_at + 1 - 2 * lax.rem(y_at, 2))
    z = lax.div(ctx, 2)
    group, me = lax.div(ctx, PEERS), lax.rem(ctx, PEERS)
    place = lax.rem(z, 4)
    far_place = lax.rem(place + 2, 4)
    facing_at = ((1 - group) * 4 + far_place) * 2 + core

    mine = lax.rem(place + 2 * group, 4)
    owns = core == 1

    def signal(sem, section, column=None):
        pl.semaphore_signal(
            sem, inc=1, device_id=(section, tp if column is None else column), device_id_type=MESH
        )

    barrier = pltpu.get_barrier_semaphore()
    for px, py in ((1, 0), (-1, 0), (0, 1), (0, -1), (2, 0), (0, 2)):
        signal(barrier, ctx, at(x + px, y_at + py))
    signal(barrier, ctx + 1 - 2 * core)

    @pl.when(z < 7)
    def _():
        signal(barrier, ctx + 2)

    @pl.when(group == 0)
    def _():
        signal(barrier, facing_at)

    weights = [
        pltpu.make_async_copy(a, b, w_sem.at[i])
        for i, (a, b) in enumerate(((wx, vx), (wbc, vbc), (wz, vz)))
    ]
    own = pltpu.make_async_copy(tok, held.at[tp], own_sem)
    own.start()
    for w in weights:
        w.start()
    pl.semaphore_wait(barrier, 7 + lax.min(z, 1) + group)

    def slot(dx, dy):
        return at(x - dx, y_at - dy)

    def piece(s, half):
        return held.at[s, pl.ds(half * HALF, HALF), :]

    def dxy(half, first, second):
        return (second, first) if half == 0 else (first, second)

    def send(half, source, direction, along, landing):
        dx, dy = dxy(half, *source)
        px, py = dxy(half, *((direction, 0) if along == 0 else (0, direction)))
        first, second = landing
        s = slot(dx, dy)
        src = tok.at[pl.ds(half * HALF, HALF), :] if all(isinstance(v, int) and v == 0 for v in source) else piece(s, half)
        pltpu.make_async_remote_copy(
            src_ref=src,
            dst_ref=piece(s, half),
            send_sem=g_send,
            recv_sem=g_recv.at[half, first * SIDE + second],
            device_id=(ctx, at(x + px, y_at + py)),
            device_id_type=MESH,
        ).start()

    def arrived(half, first, second):
        p = piece(slot(*dxy(half, first, second)), half)
        pltpu.make_async_copy(p, p, g_recv.at[half, first * SIDE + second]).wait()

    def along_second(half, first):
        if first == 3:

            @pl.when(core == 0)
            def _():
                send(half, (first, 0), 2, 1, (first, 2))

        send(half, (first, 0), 1, 1, (first, 1))
        send(half, (first, 0), -1, 1, (first, 3))

    def across_second(half, first):
        flag = lax.rem(first + core, 2)

        @pl.when(jnp.logical_or(core == 1, first < 3))
        def _():
            send(half, (first, 1 + 2 * flag), 1 - 2 * flag, 1, (first, 2))

    def multiply(dx, dy, begin=False):
        s = slot(dx, dy)
        a = held[s]
        depth = pl.ds(pl.multiple_of(s * FEAT, FEAT), FEAT)
        for acc, v in ((acc_x, vx), (acc_bc, vbc)):
            part = dot(a, v[depth, :])
            acc[...] = part if begin else acc[...] + part

    def multiply_all(count, offsets):
        def body(i, c):
            multiply(*offsets(i))
            return c

        lax.fori_loop(0, count, body, 0)

    for half in (0, 1):
        send(half, (0, 0), 2, 0, (2, 0))
    for half in (0, 1):
        send(half, (0, 0), 1, 0, (1, 0))
        send(half, (0, 0), -1, 0, (3, 0))
    for half in (0, 1):
        along_second(half, 0)

    @pl.when(group == 1)
    def _():
        signal(facing, facing_at)

    @pl.when(place == 3)
    def _():
        signal(up, ctx - 2)

    def sweep_up(at_place):
        @pl.when(place == at_place)
        def _():
            pl.semaphore_wait(up, 1)
            if at_place == 0:
                signal(down, ctx + 2)

        @pl.when(jnp.logical_and(place == at_place, z > 0))
        def _():
            signal(up, ctx - 2)

    def sweep_down(at_place):
        @pl.when(place == at_place)
        def _():
            pl.semaphore_wait(down, 1)
            if at_place < 3:
                signal(down, ctx + 2)

    i0 = lax.broadcasted_iota(jnp.int32, (ROWS, ROWS), 0)
    i1 = lax.broadcasted_iota(jnp.int32, (ROWS, ROWS), 1)
    upper = (i0 <= i1).astype(F32)
    cum_t = dot(decay_t[...], upper, precision=lax.Precision.HIGHEST)
    lane = lax.broadcasted_iota(jnp.int32, (1, 128), 1)
    for t in range(LT):
        rows = jnp.concatenate(
            [jnp.broadcast_to(cum_t[2 * t + k : 2 * t + k + 1], (64, ROWS)) for k in (0, 1)], 0
        )
        cum = rows.T
        total = cum[ROWS - 1 : ROWS]
        step_row = jnp.where(lane < 64, step[2 * t], step[2 * t + 1])
        grow[t] = jnp.exp(cum)
        end_w[t] = jnp.exp(total - cum) * step_row
        tot_out[t] = jnp.broadcast_to(jnp.exp(total), (8, 128))

    for half in (0, 1):
        arrived(half, 2, 0)
        along_second(half, 2)
    for half in (0, 1):
        arrived(half, 1, 0)
        along_second(half, 1)
        arrived(half, 3, 0)
        along_second(half, 3)
    for h in range(8):
        if h == 4:
            for half in (0, 1):
                arrived(half, 0, 1)
                arrived(half, 0, 3)
                across_second(half, 0)
        row = cum_t[h : h + 1]
        col = jnp.broadcast_to(row, (128, ROWS)).T
        col = jnp.concatenate([col, col], axis=1)
        keep = i0 >= i1
        seg[h] = jnp.where(keep, jnp.exp(jnp.where(keep, col - row, 0.0)), 0.0) * step[h]

    for half in (0, 1):
        arrived(half, 2, 1)
        arrived(half, 2, 3)
        across_second(half, 2)
    own.wait()
    weights[0].wait()
    weights[1].wait()
    multiply(0, 0, True)

    def beside(i):
        o, swap = 1 + 2 * lax.rem(i, 2), lax.div(i, 2)
        return swap * o, (1 - swap) * o

    multiply_all(4, beside)
    sweep_up(2)
    for half in (0, 1):
        arrived(half, 1, 1)
        arrived(half, 1, 3)
        across_second(half, 1)
    for half in (0, 1):
        arrived(half, 3, 1)
        arrived(half, 3, 3)
        across_second(half, 3)
    sweep_up(1)
    multiply_all(4, lambda i: (1 + 2 * lax.rem(i, 2), 1 + 2 * lax.div(i, 2)))
    sweep_up(0)
    for half in (0, 1):
        arrived(half, 0, 2)
    multiply_all(2, lambda i: (2 * (1 - i), 2 * i))
    sweep_down(1)
    for half in (0, 1):
        arrived(half, 1, 2)
        arrived(half, 3, 2)

    def far(i):
        o, swap = 1 + 2 * lax.rem(i, 2), lax.div(i, 2)
        return o + swap * (2 - o), 2 + swap * (o - 2)

    multiply_all(4, far)
    sweep_down(2)
    for half in (0, 1):
        arrived(half, 2, 2)
    multiply(2, 2)
    sweep_down(3)

    def before_conv(t, rows):
        p = acc_bc[rows] if t == LT else acc_x[rows, t * 128 : (t + 1) * 128]
        return p.astype(BF16)

    for t in range(LT + 1):
        rim_out[t] = before_conv(t, slice(ROWS - 16, ROWS))
    rim = pltpu.make_async_remote_copy(
        src_ref=rim_out,
        dst_ref=rim_in,
        send_sem=rim_sem.at[0],
        recv_sem=rim_sem.at[1],
        device_id=(lax.min(ctx + 1, SECTIONS - 1), tp),
        device_id_type=MESH,
    )

    @pl.when(z == 3)
    def _():
        pl.semaphore_wait(up, 1)

    @pl.when(ctx < SECTIONS - 1)
    def _():
        rim.start()

    for t in range(LT + 1):
        pre[t, 8 : 8 + ROWS] = before_conv(t, slice(0, ROWS)).astype(F32)
    def to_owners(send_one):
        def body(i, c):
            p = lax.rem(place + i, 4)
            send_one(lax.rem(p + 2 * group, 4), group * PEERS + 2 * p + 1)
            return c

        lax.fori_loop(1, 4, body, 0)

        @pl.when(core == 0)
        def _():
            send_one(mine, ctx + 1)

    def send_total(piece_of, section):
        pltpu.make_async_remote_copy(
            src_ref=tot_out.at[piece_of],
            dst_ref=tot_in.at[me],
            send_sem=tot_send,
            recv_sem=tot_recv,
            device_id=(section, tp),
            device_id_type=MESH,
        ).start()

    def send_state(piece_of, section):
        pltpu.make_async_remote_copy(
            src_ref=st_out.at[piece_of],
            dst_ref=st_in.at[me],
            send_sem=st_send,
            recv_sem=st_recv.at[me],
            device_id=(section, tp),
            device_id_type=MESH,
        ).start()

    to_owners(send_total)

    @pl.when(ctx == 0)
    def _():
        rim_in[...] = jnp.zeros_like(rim_in)

    @pl.when(ctx > 0)
    def _():
        rim.wait_recv()

    def conv(t):
        pre[t, 0:8] = rim_in[t].astype(F32)[8:]
        cols = slice(0, 128) if t == LT else slice(t * 128, (t + 1) * 128)
        taps, bias = (conv_bc, bias_bc) if t == LT else (conv_x, bias_x)
        total = bias[:, cols] + jnp.zeros((ROWS, 128), F32)
        for k in range(TAPS):
            total = total + taps[k : k + 1, cols] * pre[t, 5 + k : 5 + k + ROWS]
        return silu(total).astype(BF16)

    side = lax.rem(tp, 2)
    bc[side] = conv(LT)
    swap = pltpu.make_async_remote_copy(
        src_ref=bc.at[side],
        dst_ref=bc.at[side],
        send_sem=bc_sem.at[0],
        recv_sem=bc_sem.at[1],
        device_id=(ctx, mate),
        device_id_type=MESH,
    )
    swap.start()
    for t in range(LT):
        xs[t] = conv(t)
    other = bc.at[1 - side]
    pltpu.make_async_copy(other, other, bc_sem.at[1]).wait()

    b_t = bc[0].astype(F32).T.astype(BF16)
    for t in range(LT):
        weighted = (xs[t].astype(F32) * end_w[t]).astype(BF16)
        st_out[t] = dot(b_t, weighted).astype(BF16)
    to_owners(send_state)

    scores = dot(bc[1], b_t)

    def intra(t):
        both = [dot((seg[2 * t + k] * scores).astype(BF16), xs[t]) for k in (0, 1)]
        skip_row = jnp.where(lane < 64, skip[2 * t], skip[2 * t + 1])
        y[t] = jnp.where(lane < 64, both[0], both[1]) + skip_row * xs[t].astype(F32)

    for t in range(LT):
        intra(t)

    def landed(ref, count, sem):
        part = ref.at[pl.ds(0, count)]
        pltpu.make_async_copy(part, part, sem).wait()

    total_of_half = pltpu.make_async_remote_copy(
        src_ref=half_out,
        dst_ref=half_in,
        send_sem=half_sem.at[0],
        recv_sem=half_sem.at[1],
        device_id=(lax.max(facing_at, PEERS), tp),
        device_id_type=MESH,
    )

    def entering_copy(q):
        return pltpu.make_async_remote_copy(
            src_ref=en_out.at[q],
            dst_ref=en_in.at[mine],
            send_sem=en_send.at[q],
            recv_sem=en_recv,
            device_id=(group * PEERS + q, tp),
            device_id_type=MESH,
        )

    def sends(q):
        return jnp.logical_and(me != q, group * PEERS + q > 0)

    def state_of(q):
        @pl.when(me != q)
        def _():
            pltpu.make_async_copy(st_in.at[q], st_in.at[q], st_recv.at[q]).wait()

        return st_in[q].astype(F32)

    def send_entering(q):
        @pl.when(sends(q))
        def _():
            entering_copy(q).start()

    @pl.when(group == 0)
    def _():
        pl.semaphore_wait(facing, 1)

    @pl.when(owns)
    def _():
        tot_in[me] = tot_out[mine]
        st_in[me] = st_out[mine]
        landed(tot_in, PEERS - 1, tot_recv)

    @pl.when(jnp.logical_and(owns, group == 0))
    def _():
        state = jnp.zeros((128, 128), F32)
        for q in range(PEERS):
            en_out[q] = state.astype(BF16)
            send_entering(q)
            state = tot_in[q][0:1] * state + state_of(q)
        half_out[...] = state.astype(BF16)

    @pl.when(jnp.logical_and(owns, group == 1))
    def _():
        state = jnp.zeros((128, 128), F32)
        left = jnp.ones((8, 128), F32)
        for q in range(PEERS):
            within[q] = state
            remains[q] = left
            state = tot_in[q][0:1] * state + state_of(q)
            left = tot_in[q] * left
        total_of_half.wait_recv()
        half = half_in[...].astype(F32)

        def body(i, c):
            q = jnp.where(place < 2, PEERS - 1 - i, i)
            en_out[q] = (within[q] + remains[q][0:1] * half).astype(BF16)
            send_entering(q)
            return c

        lax.fori_loop(0, PEERS, body, 0)

    @pl.when(owns)
    def _():
        en_in[mine] = en_out[me]

    @pl.when(jnp.logical_and(owns, group == 0))
    def _():
        total_of_half.start()

    weights[2].wait()
    acc_z[...] = jnp.zeros_like(acc_z)

    def gate(i, c):
        total = acc_z[...]
        for k in range(4):
            depth = pl.ds(pl.multiple_of((4 * i + k) * FEAT, FEAT), FEAT)
            total = total + dot(held[4 * i + k], vz[depth, :])
        acc_z[...] = total
        return c

    lax.fori_loop(0, 4, gate, 0)
    for t in range(LT):
        g = acc_z[:, t * 128 : (t + 1) * 128].astype(BF16).astype(F32)
        acc_z[:, t * 128 : (t + 1) * 128] = silu(g)

    @pl.when(ctx == 0)
    def _():
        en_in[...] = jnp.zeros_like(en_in)

    @pl.when(owns)
    def _():
        landed(en_in, 3, en_recv)

    @pl.when(jnp.logical_and(ctx > 0, core == 0))
    def _():
        landed(en_in, 4, en_recv)

    squares = jnp.zeros((ROWS, 128), F32)
    for t in range(LT):
        entering = en_in[t]
        gated = (y[t] + grow[t] * dot(bc[1], entering)) * acc_z[:, t * 128 : (t + 1) * 128]
        squares = squares + gated * gated
        y[t] = gated
    local = jnp.sum(squares.T, axis=0, keepdims=True)
    sq_out[...] = jnp.broadcast_to(local, (8, ROWS))
    norm = pltpu.make_async_remote_copy(
        src_ref=sq_out,
        dst_ref=sq_in,
        send_sem=sq_sem.at[0],
        recv_sem=sq_sem.at[1],
        device_id=(ctx, mate),
        device_id_type=MESH,
    )
    norm.start()
    norm.wait_recv()
    mean = (sq_out[0:1] + sq_in[0:1]) * (1.0 / (2 * LT * 128))
    scale = jnp.broadcast_to(lax.rsqrt(mean + 1e-5), (128, ROWS)).T
    for t in range(LT):
        cols = slice(t * 128, (t + 1) * 128)
        out[:, cols] = (y[t] * scale * gain[:, cols]).astype(BF16)

    norm.wait_send()
    swap.wait_send()
    landed(held, 15, g_send)

    @pl.when(owns)
    def _():
        landed(tot_out, 3, tot_send)
        landed(st_out, 3, st_send)

    @pl.when(core == 0)
    def _():
        landed(tot_out, 4, tot_send)
        landed(st_out, 4, st_send)

    @pl.when(ctx < SECTIONS - 1)
    def _():
        rim.wait_send()

    @pl.when(jnp.logical_and(owns, group == 0))
    def _():
        total_of_half.wait_send()

    for q in range(PEERS):

        @pl.when(jnp.logical_and(owns, sends(q)))
        def _(q=q):
            entering_copy(q).wait_send()


def local(tokens, w_z, w_x, w_bc, conv_x, conv_bc, bias_x, bias_bc, decay, step, skip, gain):
    hbm = pl.BlockSpec(memory_space=pl.ANY)
    vmem = pl.BlockSpec(memory_space=pltpu.VMEM)
    smem = pl.BlockSpec(memory_space=pltpu.SMEM)
    width = w_x.shape[1]
    dma = pltpu.SemaphoreType.DMA
    scratch = [
        pltpu.VMEM((16, ROWS, FEAT), BF16),
        pltpu.VMEM(w_z.shape, BF16),
        pltpu.VMEM(w_x.shape, BF16),
        pltpu.VMEM(w_bc.shape, BF16),
        pltpu.VMEM((ROWS, width), F32),
        pltpu.VMEM((ROWS, width), F32),
        pltpu.VMEM((ROWS, 128), F32),
        pltpu.VMEM((LT + 1, 8 + ROWS, 128), F32),
        pltpu.VMEM((LT + 1, 16, 128), BF16),
        pltpu.VMEM((LT + 1, 16, 128), BF16),
        pltpu.VMEM((LT, ROWS, 128), BF16),
        pltpu.VMEM((2, ROWS, 128), BF16),
        pltpu.VMEM((8, ROWS, ROWS), F32),
        pltpu.VMEM((LT, ROWS, 128), F32),
        pltpu.VMEM((LT, ROWS, 128), F32),
        pltpu.VMEM((LT, 8, 128), F32),
        pltpu.VMEM((PEERS, 8, 128), F32),
        pltpu.VMEM((LT, 128, 128), BF16),
        pltpu.VMEM((PEERS, 128, 128), BF16),
        pltpu.VMEM((PEERS, 128, 128), BF16),
        pltpu.VMEM((LT, 128, 128), BF16),
        pltpu.VMEM((128, 128), BF16),
        pltpu.VMEM((128, 128), BF16),
        pltpu.VMEM((PEERS, 128, 128), F32),
        pltpu.VMEM((PEERS, 8, 128), F32),
        pltpu.VMEM((LT, ROWS, 128), F32),
        pltpu.VMEM((8, ROWS), F32),
        pltpu.VMEM((8, ROWS), F32),
        dma((3,)),
        dma,
        dma,
        dma((2, 16)),
        dma,
        dma,
        dma((2,)),
        dma((2,)),
        dma,
        dma((PEERS,)),
        dma((PEERS,)),
        dma,
        dma((2,)),
        dma((2,)),
        pltpu.SemaphoreType.REGULAR,
        pltpu.SemaphoreType.REGULAR,
        pltpu.SemaphoreType.REGULAR,
    ]
    return pl.pallas_call(
        kernel,
        out_shape=pltpu.VMEM((ROWS, width), BF16),
        in_specs=[hbm] * 4 + [vmem] * 5 + [smem] * 2 + [vmem],
        out_specs=vmem,
        scratch_shapes=scratch,
        compiler_params=pltpu.CompilerParams(
            collective_id=0, has_side_effects=True, vmem_limit_bytes=56 * 2**20
        ),
    )(
        tokens, w_z, w_x, w_bc, conv_x, conv_bc, bias_x.reshape(1, -1), bias_bc.reshape(1, -1),
        decay.T, step, skip, gain.reshape(1, -1),
    )


def solution(mesh):
    return jax.shard_map(
        local,
        mesh=mesh,
        in_specs=(
            P("ctx", "tp"),
            P(None, "tp"),
            P(None, "tp"),
            P(None, "tp"),
            P(None, "tp"),
            P(None, "tp"),
            P("tp"),
            P("tp"),
            P("ctx", "tp"),
            P("tp"),
            P("tp"),
            P("tp"),
        ),
        out_specs=P("ctx", "tp"),
        check_vma=False,
    )
```

```python
import jax
import jax.numpy as jnp
from jax import lax
from jax.experimental import pallas as pl
from jax.experimental.pallas import tpu as pltpu
from jax.sharding import PartitionSpec as P

MESH = pl.DeviceIdType.MESH
SIDE = 4
TAPS = 4
ROWS = 256
HALF = 128
FEAT = 256
SECTIONS = 16
PEERS = 8
LT = 4
F32 = jnp.float32
BF16 = jnp.bfloat16


def silu(v):
    return v / (1.0 + jnp.exp(-v))


def dot(a, b, **kw):
    return jnp.dot(a, b, preferred_element_type=F32, **kw)


def kernel(
    tok, wz, wx, wbc, conv_x, conv_bc, bias_x, bias_bc, decay_t, step, skip, gain, out,
    held, vz, vx, vbc, acc_z, acc_x, acc_bc, pre, rim_out, rim_in, xs, bc, seg, grow, end_w,
    tot_out, tot_in, st_out, st_in, en_out, en_in, half_out, half_in, within, remains, y, sq_out, sq_in,
    w_sem, own_sem, g_send, g_recv, tot_send, tot_recv, rim_sem, bc_sem, st_send, st_recv,
    en_send, en_recv, half_sem, sq_sem, up, down, facing,
):
    ctx, tp = lax.axis_index("ctx"), lax.axis_index("tp")
    core = lax.rem(ctx, 2)
    x, y_at = lax.div(tp, SIDE), lax.rem(tp, SIDE)

    def at(px, py):
        return lax.rem(px + 2 * SIDE, SIDE) * SIDE + lax.rem(py + 2 * SIDE, SIDE)

    mate = at(x, y_at + 1 - 2 * lax.rem(y_at, 2))
    z = lax.div(ctx, 2)
    group, me = lax.div(ctx, PEERS), lax.rem(ctx, PEERS)
    place = lax.rem(z, 4)
    far_place = lax.rem(place + 2, 4)
    facing_at = ((1 - group) * 4 + far_place) * 2 + core

    mine = lax.rem(place + 2 * group, 4)
    owns = core == 1

    def signal(sem, section, column=None):
        pl.semaphore_signal(
            sem, inc=1, device_id=(section, tp if column is None else column), device_id_type=MESH
        )

    barrier = pltpu.get_barrier_semaphore()
    for px, py in ((1, 0), (-1, 0), (0, 1), (0, -1), (2, 0), (0, 2)):
        signal(barrier, ctx, at(x + px, y_at + py))
    signal(barrier, ctx + 1 - 2 * core)

    @pl.when(z < 7)
    def _():
        signal(barrier, ctx + 2)

    @pl.when(group == 0)
    def _():
        signal(barrier, facing_at)

    weights = [
        pltpu.make_async_copy(a, b, w_sem.at[i])
        for i, (a, b) in enumerate(((wx, vx), (wbc, vbc), (wz, vz)))
    ]
    own = pltpu.make_async_copy(tok, held.at[tp], own_sem)
    own.start()
    for w in weights:
        w.start()
    pl.semaphore_wait(barrier, 7 + lax.min(z, 1) + group)

    def slot(dx, dy):
        return at(x - dx, y_at - dy)

    def piece(s, half):
        return held.at[s, pl.ds(half * HALF, HALF), :]

    def dxy(half, first, second):
        return (second, first) if half == 0 else (first, second)

    def send(half, source, direction, along, landing):
        dx, dy = dxy(half, *source)
        px, py = dxy(half, *((direction, 0) if along == 0 else (0, direction)))
        first, second = landing
        s = slot(dx, dy)
        src = tok.at[pl.ds(half * HALF, HALF), :] if all(isinstance(v, int) and v == 0 for v in source) else piece(s, half)
        pltpu.make_async_remote_copy(
            src_ref=src,
            dst_ref=piece(s, half),
            send_sem=g_send,
            recv_sem=g_recv.at[half, first * SIDE + second],
            device_id=(ctx, at(x + px, y_at + py)),
            device_id_type=MESH,
        ).start()

    def arrived(half, first, second):
        p = piece(slot(*dxy(half, first, second)), half)
        pltpu.make_async_copy(p, p, g_recv.at[half, first * SIDE + second]).wait()

    def along_second(half, first):
        if first == 3:

            @pl.when(core == 0)
            def _():
                send(half, (first, 0), 2, 1, (first, 2))

        send(half, (first, 0), 1, 1, (first, 1))
        send(half, (first, 0), -1, 1, (first, 3))

    def across_second(half, first):
        flag = lax.rem(first + core, 2)

        @pl.when(jnp.logical_or(core == 1, first < 3))
        def _():
            send(half, (first, 1 + 2 * flag), 1 - 2 * flag, 1, (first, 2))

    def multiply(dx, dy, begin=False):
        s = slot(dx, dy)
        a = held[s]
        depth = pl.ds(pl.multiple_of(s * FEAT, FEAT), FEAT)
        for acc, v in ((acc_x, vx), (acc_bc, vbc)):
            part = dot(a, v[depth, :])
            acc[...] = part if begin else acc[...] + part

    def multiply_all(count, offsets):
        def body(i, c):
            multiply(*offsets(i))
            return c

        lax.fori_loop(0, count, body, 0)

    for half in (0, 1):
        send(half, (0, 0), 2, 0, (2, 0))
    for half in (0, 1):
        send(half, (0, 0), 1, 0, (1, 0))
        send(half, (0, 0), -1, 0, (3, 0))
    for half in (0, 1):
        along_second(half, 0)

    @pl.when(group == 1)
    def _():
        signal(facing, facing_at)

    @pl.when(place == 3)
    def _():
        signal(up, ctx - 2)

    def sweep_up(at_place):
        @pl.when(place == at_place)
        def _():
            pl.semaphore_wait(up, 1)
            if at_place == 0:
                signal(down, ctx + 2)

        @pl.when(jnp.logical_and(place == at_place, z > 0))
        def _():
            signal(up, ctx - 2)

    def sweep_down(at_place):
        @pl.when(place == at_place)
        def _():
            pl.semaphore_wait(down, 1)
            if at_place < 3:
                signal(down, ctx + 2)

    i0 = lax.broadcasted_iota(jnp.int32, (ROWS, ROWS), 0)
    i1 = lax.broadcasted_iota(jnp.int32, (ROWS, ROWS), 1)
    upper = (i0 <= i1).astype(F32)
    cum_t = dot(decay_t[...], upper, precision=lax.Precision.HIGHEST)
    lane = lax.broadcasted_iota(jnp.int32, (1, 128), 1)
    for t in range(LT):
        rows = jnp.concatenate(
            [jnp.broadcast_to(cum_t[2 * t + k : 2 * t + k + 1], (64, ROWS)) for k in (0, 1)], 0
        )
        cum = rows.T
        total = cum[ROWS - 1 : ROWS]
        step_row = jnp.where(lane < 64, step[2 * t], step[2 * t + 1])
        grow[t] = jnp.exp(cum)
        end_w[t] = jnp.exp(total - cum) * step_row
        tot_out[t] = jnp.broadcast_to(jnp.exp(total), (8, 128))

    for half in (0, 1):
        arrived(half, 2, 0)
        along_second(half, 2)
    for half in (0, 1):
        arrived(half, 1, 0)
        along_second(half, 1)
        arrived(half, 3, 0)
        along_second(half, 3)
    for h in range(8):
        if h == 4:
            for half in (0, 1):
                arrived(half, 0, 1)
                arrived(half, 0, 3)
                across_second(half, 0)
        row = cum_t[h : h + 1]
        col = jnp.broadcast_to(row, (128, ROWS)).T
        col = jnp.concatenate([col, col], axis=1)
        keep = i0 >= i1
        seg[h] = jnp.where(keep, jnp.exp(jnp.where(keep, col - row, 0.0)), 0.0) * step[h]

    for half in (0, 1):
        arrived(half, 2, 1)
        arrived(half, 2, 3)
        across_second(half, 2)
    own.wait()
    weights[0].wait()
    weights[1].wait()
    multiply(0, 0, True)

    def beside(i):
        o, swap = 1 + 2 * lax.rem(i, 2), lax.div(i, 2)
        return swap * o, (1 - swap) * o

    multiply_all(4, beside)
    sweep_up(2)
    for half in (0, 1):
        arrived(half, 1, 1)
        arrived(half, 1, 3)
        across_second(half, 1)
    for half in (0, 1):
        arrived(half, 3, 1)
        arrived(half, 3, 3)
        across_second(half, 3)
    sweep_up(1)
    multiply_all(4, lambda i: (1 + 2 * lax.rem(i, 2), 1 + 2 * lax.div(i, 2)))
    sweep_up(0)
    for half in (0, 1):
        arrived(half, 0, 2)
    multiply_all(2, lambda i: (2 * (1 - i), 2 * i))
    sweep_down(1)
    for half in (0, 1):
        arrived(half, 1, 2)
        arrived(half, 3, 2)

    def far(i):
        o, swap = 1 + 2 * lax.rem(i, 2), lax.div(i, 2)
        return o + swap * (2 - o), 2 + swap * (o - 2)

    multiply_all(4, far)
    sweep_down(2)
    for half in (0, 1):
        arrived(half, 2, 2)
    multiply(2, 2)
    sweep_down(3)

    def before_conv(t, rows):
        p = acc_bc[rows] if t == LT else acc_x[rows, t * 128 : (t + 1) * 128]
        return p.astype(BF16)

    for t in range(LT + 1):
        rim_out[t] = before_conv(t, slice(ROWS - 16, ROWS))
    rim = pltpu.make_async_remote_copy(
        src_ref=rim_out,
        dst_ref=rim_in,
        send_sem=rim_sem.at[0],
        recv_sem=rim_sem.at[1],
        device_id=(lax.min(ctx + 1, SECTIONS - 1), tp),
        device_id_type=MESH,
    )

    @pl.when(z == 3)
    def _():
        pl.semaphore_wait(up, 1)

    @pl.when(ctx < SECTIONS - 1)
    def _():
        rim.start()

    for t in range(LT + 1):
        pre[t, 8 : 8 + ROWS] = before_conv(t, slice(0, ROWS)).astype(F32)
    def to_owners(send_one):
        def body(i, c):
            p = lax.rem(place + i, 4)
            send_one(lax.rem(p + 2 * group, 4), group * PEERS + 2 * p + 1)
            return c

        lax.fori_loop(1, 4, body, 0)

        @pl.when(core == 0)
        def _():
            send_one(mine, ctx + 1)

    def send_total(piece_of, section):
        pltpu.make_async_remote_copy(
            src_ref=tot_out.at[piece_of],
            dst_ref=tot_in.at[me],
            send_sem=tot_send,
            recv_sem=tot_recv,
            device_id=(section, tp),
            device_id_type=MESH,
        ).start()

    def send_state(piece_of, section):
        pltpu.make_async_remote_copy(
            src_ref=st_out.at[piece_of],
            dst_ref=st_in.at[me],
            send_sem=st_send,
            recv_sem=st_recv.at[me],
            device_id=(section, tp),
            device_id_type=MESH,
        ).start()

    def conv(t, low, high):
        cols = slice(0, 128) if t == LT else slice(t * 128, (t + 1) * 128)
        taps, bias = (conv_bc, bias_bc) if t == LT else (conv_x, bias_x)
        total = bias[:, cols] + jnp.zeros((high - low, 128), F32)
        for k in range(TAPS):
            total = total + taps[k : k + 1, cols] * pre[t, 5 + k + low : 5 + k + high]
        return silu(total).astype(BF16)

    side = lax.rem(tp, 2)

    def swap(which, low, high):
        part = bc.at[side, pl.ds(low, high - low)]
        return pltpu.make_async_remote_copy(
            src_ref=part,
            dst_ref=part,
            send_sem=bc_sem.at[0, which],
            recv_sem=bc_sem.at[1, which],
            device_id=(ctx, mate),
            device_id_type=MESH,
        )

    most, first_rows = swap(0, 16, ROWS), swap(1, 0, 16)
    bc[side, 16:ROWS] = conv(LT, 16, ROWS)
    most.start()
    for t in range(LT):
        xs[t, 16:ROWS] = conv(t, 16, ROWS)
    to_owners(send_total)

    @pl.when(ctx == 0)
    def _():
        rim_in[...] = jnp.zeros_like(rim_in)

    @pl.when(ctx > 0)
    def _():
        rim.wait_recv()

    for t in range(LT + 1):
        pre[t, 0:8] = rim_in[t].astype(F32)[8:]
    bc[side, 0:16] = conv(LT, 0, 16)
    first_rows.start()
    for t in range(LT):
        xs[t, 0:16] = conv(t, 0, 16)
    for which, low, high in ((0, 16, ROWS), (1, 0, 16)):
        other = bc.at[1 - side, pl.ds(low, high - low)]
        pltpu.make_async_copy(other, other, bc_sem.at[1, which]).wait()

    b_t = bc[0].astype(F32).T.astype(BF16)
    for t in range(LT):
        weighted = (xs[t].astype(F32) * end_w[t]).astype(BF16)
        st_out[t] = dot(b_t, weighted).astype(BF16)
    to_owners(send_state)

    scores = dot(bc[1], b_t)

    def intra(t):
        both = [dot((seg[2 * t + k] * scores).astype(BF16), xs[t]) for k in (0, 1)]
        skip_row = jnp.where(lane < 64, skip[2 * t], skip[2 * t + 1])
        y[t] = jnp.where(lane < 64, both[0], both[1]) + skip_row * xs[t].astype(F32)

    for t in range(LT):
        intra(t)

    def landed(ref, count, sem):
        part = ref.at[pl.ds(0, count)]
        pltpu.make_async_copy(part, part, sem).wait()

    total_of_half = pltpu.make_async_remote_copy(
        src_ref=half_out,
        dst_ref=half_in,
        send_sem=half_sem.at[0],
        recv_sem=half_sem.at[1],
        device_id=(lax.max(facing_at, PEERS), tp),
        device_id_type=MESH,
    )

    def entering_copy(q):
        return pltpu.make_async_remote_copy(
            src_ref=en_out.at[q],
            dst_ref=en_in.at[mine],
            send_sem=en_send.at[q],
            recv_sem=en_recv,
            device_id=(group * PEERS + q, tp),
            device_id_type=MESH,
        )

    def sends(q):
        return jnp.logical_and(me != q, group * PEERS + q > 0)

    def state_of(q):
        @pl.when(me != q)
        def _():
            pltpu.make_async_copy(st_in.at[q], st_in.at[q], st_recv.at[q]).wait()

        return st_in[q].astype(F32)

    def send_entering(q):
        @pl.when(sends(q))
        def _():
            entering_copy(q).start()

    @pl.when(group == 0)
    def _():
        pl.semaphore_wait(facing, 1)

    @pl.when(owns)
    def _():
        tot_in[me] = tot_out[mine]
        st_in[me] = st_out[mine]
        landed(tot_in, PEERS - 1, tot_recv)

    @pl.when(jnp.logical_and(owns, group == 0))
    def _():
        state = jnp.zeros((128, 128), F32)
        for q in range(PEERS):
            en_out[q] = state.astype(BF16)
            send_entering(q)
            state = tot_in[q][0:1] * state + state_of(q)
        half_out[...] = state.astype(BF16)

    @pl.when(jnp.logical_and(owns, group == 1))
    def _():
        state = jnp.zeros((128, 128), F32)
        left = jnp.ones((8, 128), F32)
        for q in range(PEERS):
            within[q] = state
            remains[q] = left
            state = tot_in[q][0:1] * state + state_of(q)
            left = tot_in[q] * left
        total_of_half.wait_recv()
        half = half_in[...].astype(F32)

        def body(i, c):
            q = jnp.where(place < 2, 2 * (3 - lax.div(i, 2)) + lax.rem(i, 2), i)
            en_out[q] = (within[q] + remains[q][0:1] * half).astype(BF16)
            send_entering(q)
            return c

        lax.fori_loop(0, PEERS, body, 0)

    @pl.when(owns)
    def _():
        en_in[mine] = en_out[me]

    @pl.when(jnp.logical_and(owns, group == 0))
    def _():
        total_of_half.start()

    weights[2].wait()
    acc_z[...] = jnp.zeros_like(acc_z)

    def gate(i, c):
        total = acc_z[...]
        for k in range(4):
            depth = pl.ds(pl.multiple_of((4 * i + k) * FEAT, FEAT), FEAT)
            total = total + dot(held[4 * i + k], vz[depth, :])
        acc_z[...] = total
        return c

    lax.fori_loop(0, 4, gate, 0)
    for t in range(LT):
        g = acc_z[:, t * 128 : (t + 1) * 128].astype(BF16).astype(F32)
        acc_z[:, t * 128 : (t + 1) * 128] = silu(g)

    @pl.when(ctx == 0)
    def _():
        en_in[...] = jnp.zeros_like(en_in)

    @pl.when(owns)
    def _():
        landed(en_in, 3, en_recv)

    @pl.when(jnp.logical_and(ctx > 0, core == 0))
    def _():
        landed(en_in, 4, en_recv)

    squares = jnp.zeros((ROWS, 128), F32)
    for t in range(LT):
        entering = en_in[t]
        gated = (y[t] + grow[t] * dot(bc[1], entering)) * acc_z[:, t * 128 : (t + 1) * 128]
        squares = squares + gated * gated
        y[t] = gated
    local = jnp.sum(squares.T, axis=0, keepdims=True)
    sq_out[...] = jnp.broadcast_to(local, (8, ROWS))
    norm = pltpu.make_async_remote_copy(
        src_ref=sq_out,
        dst_ref=sq_in,
        send_sem=sq_sem.at[0],
        recv_sem=sq_sem.at[1],
        device_id=(ctx, mate),
        device_id_type=MESH,
    )
    norm.start()
    norm.wait_recv()
    mean = (sq_out[0:1] + sq_in[0:1]) * (1.0 / (2 * LT * 128))
    scale = jnp.broadcast_to(lax.rsqrt(mean + 1e-5), (128, ROWS)).T
    for t in range(LT):
        cols = slice(t * 128, (t + 1) * 128)
        out[:, cols] = (y[t] * scale * gain[:, cols]).astype(BF16)

    norm.wait_send()
    most.wait_send()
    first_rows.wait_send()
    landed(held, 15, g_send)

    @pl.when(owns)
    def _():
        landed(tot_out, 3, tot_send)
        landed(st_out, 3, st_send)

    @pl.when(core == 0)
    def _():
        landed(tot_out, 4, tot_send)
        landed(st_out, 4, st_send)

    @pl.when(ctx < SECTIONS - 1)
    def _():
        rim.wait_send()

    @pl.when(jnp.logical_and(owns, group == 0))
    def _():
        total_of_half.wait_send()

    for q in range(PEERS):

        @pl.when(jnp.logical_and(owns, sends(q)))
        def _(q=q):
            entering_copy(q).wait_send()


def local(tokens, w_z, w_x, w_bc, conv_x, conv_bc, bias_x, bias_bc, decay, step, skip, gain):
    hbm = pl.BlockSpec(memory_space=pl.ANY)
    vmem = pl.BlockSpec(memory_space=pltpu.VMEM)
    smem = pl.BlockSpec(memory_space=pltpu.SMEM)
    width = w_x.shape[1]
    dma = pltpu.SemaphoreType.DMA
    scratch = [
        pltpu.VMEM((16, ROWS, FEAT), BF16),
        pltpu.VMEM(w_z.shape, BF16),
        pltpu.VMEM(w_x.shape, BF16),
        pltpu.VMEM(w_bc.shape, BF16),
        pltpu.VMEM((ROWS, width), F32),
        pltpu.VMEM((ROWS, width), F32),
        pltpu.VMEM((ROWS, 128), F32),
        pltpu.VMEM((LT + 1, 8 + ROWS, 128), F32),
        pltpu.VMEM((LT + 1, 16, 128), BF16),
        pltpu.VMEM((LT + 1, 16, 128), BF16),
        pltpu.VMEM((LT, ROWS, 128), BF16),
        pltpu.VMEM((2, ROWS, 128), BF16),
        pltpu.VMEM((8, ROWS, ROWS), F32),
        pltpu.VMEM((LT, ROWS, 128), F32),
        pltpu.VMEM((LT, ROWS, 128), F32),
        pltpu.VMEM((LT, 8, 128), F32),
        pltpu.VMEM((PEERS, 8, 128), F32),
        pltpu.VMEM((LT, 128, 128), BF16),
        pltpu.VMEM((PEERS, 128, 128), BF16),
        pltpu.VMEM((PEERS, 128, 128), BF16),
        pltpu.VMEM((LT, 128, 128), BF16),
        pltpu.VMEM((128, 128), BF16),
        pltpu.VMEM((128, 128), BF16),
        pltpu.VMEM((PEERS, 128, 128), F32),
        pltpu.VMEM((PEERS, 8, 128), F32),
        pltpu.VMEM((LT, ROWS, 128), F32),
        pltpu.VMEM((8, ROWS), F32),
        pltpu.VMEM((8, ROWS), F32),
        dma((3,)),
        dma,
        dma,
        dma((2, 16)),
        dma,
        dma,
        dma((2,)),
        dma((2, 2)),
        dma,
        dma((PEERS,)),
        dma((PEERS,)),
        dma,
        dma((2,)),
        dma((2,)),
        pltpu.SemaphoreType.REGULAR,
        pltpu.SemaphoreType.REGULAR,
        pltpu.SemaphoreType.REGULAR,
    ]
    return pl.pallas_call(
        kernel,
        out_shape=pltpu.VMEM((ROWS, width), BF16),
        in_specs=[hbm] * 4 + [vmem] * 5 + [smem] * 2 + [vmem],
        out_specs=vmem,
        scratch_shapes=scratch,
        compiler_params=pltpu.CompilerParams(
            collective_id=0, has_side_effects=True, vmem_limit_bytes=56 * 2**20
        ),
    )(
        tokens, w_z, w_x, w_bc, conv_x, conv_bc, bias_x.reshape(1, -1), bias_bc.reshape(1, -1),
        decay.T, step, skip, gain.reshape(1, -1),
    )


def solution(mesh):
    return jax.shard_map(
        local,
        mesh=mesh,
        in_specs=(
            P("ctx", "tp"),
            P(None, "tp"),
            P(None, "tp"),
            P(None, "tp"),
            P(None, "tp"),
            P(None, "tp"),
            P("tp"),
            P("tp"),
            P("ctx", "tp"),
            P("tp"),
            P("tp"),
            P("tp"),
        ),
        out_specs=P("ctx", "tp"),
        check_vma=False,
    )
```

```python
import jax
import jax.numpy as jnp
from jax import lax
from jax.experimental import pallas as pl
from jax.experimental.pallas import tpu as pltpu
from jax.sharding import PartitionSpec as P

MESH = pl.DeviceIdType.MESH
SIDE = 4
TAPS = 4
ROWS = 256
HALF = 128
FEAT = 256
SECTIONS = 16
PEERS = 8
LT = 4
F32 = jnp.float32
BF16 = jnp.bfloat16


def silu(v):
    return v / (1.0 + jnp.exp(-v))


def dot(a, b, **kw):
    return jnp.dot(a, b, preferred_element_type=F32, **kw)


def kernel(
    tok, wz, wx, wbc, conv_x, conv_bc, bias_x, bias_bc, decay_t, step, skip, gain, out,
    held, vz, vx, vbc, acc_z, acc_x, acc_bc, pre, rim_out, rim_in, xs, bc, seg, grow, end_w,
    tot_out, tot_in, st_out, st_in, en_out, en_in, half_out, half_in, within, remains, mate_st, mate_tot, y, sq_out, sq_in,
    w_sem, own_sem, g_send, g_recv, tot_send, tot_recv, rim_sem, bc_sem, st_send, st_recv,
    en_send, en_recv, half_sem, sq_sem, pair_sem, up, down, facing,
):
    ctx, tp = lax.axis_index("ctx"), lax.axis_index("tp")
    core = lax.rem(ctx, 2)
    x, y_at = lax.div(tp, SIDE), lax.rem(tp, SIDE)

    def at(px, py):
        return lax.rem(px + 2 * SIDE, SIDE) * SIDE + lax.rem(py + 2 * SIDE, SIDE)

    mate = at(x, y_at + 1 - 2 * lax.rem(y_at, 2))
    z = lax.div(ctx, 2)
    group, me = lax.div(ctx, PEERS), lax.rem(ctx, PEERS)
    place = lax.rem(z, 4)
    far_place = lax.rem(place + 2, 4)
    facing_at = ((1 - group) * 4 + far_place) * 2 + core

    mine = lax.rem(place + 2 * group, 4)
    owns = core == 1

    def signal(sem, section, column=None):
        pl.semaphore_signal(
            sem, inc=1, device_id=(section, tp if column is None else column), device_id_type=MESH
        )

    barrier = pltpu.get_barrier_semaphore()
    for px, py in ((1, 0), (-1, 0), (0, 1), (0, -1), (2, 0), (0, 2)):
        signal(barrier, ctx, at(x + px, y_at + py))
    signal(barrier, ctx + 1 - 2 * core)

    @pl.when(z < 7)
    def _():
        signal(barrier, ctx + 2)

    @pl.when(group == 0)
    def _():
        signal(barrier, facing_at)

    weights = [
        pltpu.make_async_copy(a, b, w_sem.at[i])
        for i, (a, b) in enumerate(((wx, vx), (wbc, vbc), (wz, vz)))
    ]
    own = pltpu.make_async_copy(tok, held.at[tp], own_sem)
    own.start()
    for w in weights:
        w.start()
    pl.semaphore_wait(barrier, 7 + lax.min(z, 1) + group)

    def slot(dx, dy):
        return at(x - dx, y_at - dy)

    def piece(s, half):
        return held.at[s, pl.ds(half * HALF, HALF), :]

    def dxy(half, first, second):
        return (second, first) if half == 0 else (first, second)

    def send(half, source, direction, along, landing):
        dx, dy = dxy(half, *source)
        px, py = dxy(half, *((direction, 0) if along == 0 else (0, direction)))
        first, second = landing
        s = slot(dx, dy)
        src = tok.at[pl.ds(half * HALF, HALF), :] if all(isinstance(v, int) and v == 0 for v in source) else piece(s, half)
        pltpu.make_async_remote_copy(
            src_ref=src,
            dst_ref=piece(s, half),
            send_sem=g_send,
            recv_sem=g_recv.at[half, first * SIDE + second],
            device_id=(ctx, at(x + px, y_at + py)),
            device_id_type=MESH,
        ).start()

    def arrived(half, first, second):
        p = piece(slot(*dxy(half, first, second)), half)
        pltpu.make_async_copy(p, p, g_recv.at[half, first * SIDE + second]).wait()

    def along_second(half, first):
        if first == 3:

            @pl.when(core == 0)
            def _():
                send(half, (first, 0), 2, 1, (first, 2))

        send(half, (first, 0), 1, 1, (first, 1))
        send(half, (first, 0), -1, 1, (first, 3))

    def across_second(half, first):
        flag = lax.rem(first + core, 2)

        @pl.when(jnp.logical_or(core == 1, first < 3))
        def _():
            send(half, (first, 1 + 2 * flag), 1 - 2 * flag, 1, (first, 2))

    def multiply(dx, dy, begin=False):
        s = slot(dx, dy)
        a = held[s]
        depth = pl.ds(pl.multiple_of(s * FEAT, FEAT), FEAT)
        for acc, v in ((acc_x, vx), (acc_bc, vbc)):
            part = dot(a, v[depth, :])
            acc[...] = part if begin else acc[...] + part

    def multiply_all(count, offsets):
        def body(i, c):
            multiply(*offsets(i))
            return c

        lax.fori_loop(0, count, body, 0)

    for half in (0, 1):
        send(half, (0, 0), 2, 0, (2, 0))
    for half in (0, 1):
        send(half, (0, 0), 1, 0, (1, 0))
        send(half, (0, 0), -1, 0, (3, 0))
    for half in (0, 1):
        along_second(half, 0)

    @pl.when(group == 1)
    def _():
        signal(facing, facing_at)

    @pl.when(place == 3)
    def _():
        signal(up, ctx - 2)

    def sweep_up(at_place):
        @pl.when(place == at_place)
        def _():
            pl.semaphore_wait(up, 1)
            if at_place == 0:
                signal(down, ctx + 2)

        @pl.when(jnp.logical_and(place == at_place, z > 0))
        def _():
            signal(up, ctx - 2)

    def sweep_down(at_place):
        @pl.when(place == at_place)
        def _():
            pl.semaphore_wait(down, 1)
            if at_place < 3:
                signal(down, ctx + 2)

    i0 = lax.broadcasted_iota(jnp.int32, (ROWS, ROWS), 0)
    i1 = lax.broadcasted_iota(jnp.int32, (ROWS, ROWS), 1)
    upper = (i0 <= i1).astype(F32)
    cum_t = dot(decay_t[...], upper, precision=lax.Precision.HIGHEST)
    lane = lax.broadcasted_iota(jnp.int32, (1, 128), 1)
    for t in range(LT):
        rows = jnp.concatenate(
            [jnp.broadcast_to(cum_t[2 * t + k : 2 * t + k + 1], (64, ROWS)) for k in (0, 1)], 0
        )
        cum = rows.T
        total = cum[ROWS - 1 : ROWS]
        step_row = jnp.where(lane < 64, step[2 * t], step[2 * t + 1])
        grow[t] = jnp.exp(cum)
        end_w[t] = jnp.exp(total - cum) * step_row
        tot_out[t] = jnp.broadcast_to(jnp.exp(total), (8, 128))

    for half in (0, 1):
        arrived(half, 2, 0)
        along_second(half, 2)
    for half in (0, 1):
        arrived(half, 1, 0)
        along_second(half, 1)
        arrived(half, 3, 0)
        along_second(half, 3)
    for h in range(8):
        if h == 4:
            for half in (0, 1):
                arrived(half, 0, 1)
                arrived(half, 0, 3)
                across_second(half, 0)
        row = cum_t[h : h + 1]
        col = jnp.broadcast_to(row, (128, ROWS)).T
        col = jnp.concatenate([col, col], axis=1)
        keep = i0 >= i1
        seg[h] = jnp.where(keep, jnp.exp(jnp.where(keep, col - row, 0.0)), 0.0) * step[h]

    for half in (0, 1):
        arrived(half, 2, 1)
        arrived(half, 2, 3)
        across_second(half, 2)
    own.wait()
    weights[0].wait()
    weights[1].wait()
    multiply(0, 0, True)

    def beside(i):
        o, swap = 1 + 2 * lax.rem(i, 2), lax.div(i, 2)
        return swap * o, (1 - swap) * o

    multiply_all(4, beside)
    sweep_up(2)
    for half in (0, 1):
        arrived(half, 1, 1)
        arrived(half, 1, 3)
        across_second(half, 1)
    for half in (0, 1):
        arrived(half, 3, 1)
        arrived(half, 3, 3)
        across_second(half, 3)
    sweep_up(1)
    multiply_all(4, lambda i: (1 + 2 * lax.rem(i, 2), 1 + 2 * lax.div(i, 2)))
    sweep_up(0)
    for half in (0, 1):
        arrived(half, 0, 2)
    multiply_all(2, lambda i: (2 * (1 - i), 2 * i))
    sweep_down(1)
    for half in (0, 1):
        arrived(half, 1, 2)
        arrived(half, 3, 2)

    def far(i):
        o, swap = 1 + 2 * lax.rem(i, 2), lax.div(i, 2)
        return o + swap * (2 - o), 2 + swap * (o - 2)

    multiply_all(4, far)
    sweep_down(2)
    for half in (0, 1):
        arrived(half, 2, 2)
    multiply(2, 2)
    sweep_down(3)

    def before_conv(t, rows):
        p = acc_bc[rows] if t == LT else acc_x[rows, t * 128 : (t + 1) * 128]
        return p.astype(BF16)

    for t in range(LT + 1):
        rim_out[t] = before_conv(t, slice(ROWS - 16, ROWS))
    rim = pltpu.make_async_remote_copy(
        src_ref=rim_out,
        dst_ref=rim_in,
        send_sem=rim_sem.at[0],
        recv_sem=rim_sem.at[1],
        device_id=(lax.min(ctx + 1, SECTIONS - 1), tp),
        device_id_type=MESH,
    )

    @pl.when(z == 3)
    def _():
        pl.semaphore_wait(up, 1)

    @pl.when(ctx < SECTIONS - 1)
    def _():
        rim.start()

    for t in range(LT + 1):
        pre[t, 8 : 8 + ROWS] = before_conv(t, slice(0, ROWS)).astype(F32)
    def to_owners(send_one):
        def body(i, c):
            p = lax.rem(place + i, 4)
            send_one(lax.rem(p + 2 * group, 4), group * PEERS + 2 * p + 1)
            return c

        lax.fori_loop(1, 4, body, 0)

        @pl.when(core == 0)
        def _():
            send_one(mine, ctx + 1)

    def send_total(piece_of, section):
        pltpu.make_async_remote_copy(
            src_ref=tot_out.at[piece_of],
            dst_ref=tot_in.at[me],
            send_sem=tot_send,
            recv_sem=tot_recv,
            device_id=(section, tp),
            device_id_type=MESH,
        ).start()

    def send_state(piece_of, section):
        pltpu.make_async_remote_copy(
            src_ref=st_out.at[piece_of],
            dst_ref=st_in.at[me],
            send_sem=st_send,
            recv_sem=st_recv.at[me],
            device_id=(section, tp),
            device_id_type=MESH,
        ).start()

    def conv(t, low, high):
        cols = slice(0, 128) if t == LT else slice(t * 128, (t + 1) * 128)
        taps, bias = (conv_bc, bias_bc) if t == LT else (conv_x, bias_x)
        total = bias[:, cols] + jnp.zeros((high - low, 128), F32)
        for k in range(TAPS):
            total = total + taps[k : k + 1, cols] * pre[t, 5 + k + low : 5 + k + high]
        return silu(total).astype(BF16)

    side = lax.rem(tp, 2)

    def swap(which, low, high):
        part = bc.at[side, pl.ds(low, high - low)]
        return pltpu.make_async_remote_copy(
            src_ref=part,
            dst_ref=part,
            send_sem=bc_sem.at[0, which],
            recv_sem=bc_sem.at[1, which],
            device_id=(ctx, mate),
            device_id_type=MESH,
        )

    most, first_rows = swap(0, 16, ROWS), swap(1, 0, 16)
    bc[side, 16:ROWS] = conv(LT, 16, ROWS)
    most.start()
    for t in range(LT):
        xs[t, 16:ROWS] = conv(t, 16, ROWS)
    to_owners(send_total)

    @pl.when(ctx == 0)
    def _():
        rim_in[...] = jnp.zeros_like(rim_in)

    @pl.when(ctx > 0)
    def _():
        rim.wait_recv()

    for t in range(LT + 1):
        pre[t, 0:8] = rim_in[t].astype(F32)[8:]
    bc[side, 0:16] = conv(LT, 0, 16)
    first_rows.start()
    for t in range(LT):
        xs[t, 0:16] = conv(t, 0, 16)
    for which, low, high in ((0, 16, ROWS), (1, 0, 16)):
        other = bc.at[1 - side, pl.ds(low, high - low)]
        pltpu.make_async_copy(other, other, bc_sem.at[1, which]).wait()

    b_t = bc[0].astype(F32).T.astype(BF16)
    for t in range(LT):
        weighted = (xs[t].astype(F32) * end_w[t]).astype(BF16)
        st_out[t] = dot(b_t, weighted).astype(BF16)
    to_owners(send_state)

    def to_pair(src, dst, which):
        return pltpu.make_async_remote_copy(
            src_ref=src,
            dst_ref=dst,
            send_sem=pair_sem.at[0, which],
            recv_sem=pair_sem.at[1, which],
            device_id=(ctx + 1 - 2 * core, tp),
            device_id_type=MESH,
        )

    pair_state = to_pair(st_out, mate_st, 0)
    pair_total = to_pair(tot_out, mate_tot, 1)
    pair_entering = to_pair(en_in, en_in, 2)

    @pl.when(core == 0)
    def _():
        pair_state.start()
        pair_total.start()


    scores = dot(bc[1], b_t)

    def intra(t):
        both = [dot((seg[2 * t + k] * scores).astype(BF16), xs[t]) for k in (0, 1)]
        skip_row = jnp.where(lane < 64, skip[2 * t], skip[2 * t + 1])
        y[t] = jnp.where(lane < 64, both[0], both[1]) + skip_row * xs[t].astype(F32)

    for t in range(LT):
        intra(t)

    def landed(ref, count, sem):
        part = ref.at[pl.ds(0, count)]
        pltpu.make_async_copy(part, part, sem).wait()

    total_of_half = pltpu.make_async_remote_copy(
        src_ref=half_out,
        dst_ref=half_in,
        send_sem=half_sem.at[0],
        recv_sem=half_sem.at[1],
        device_id=(lax.max(facing_at, PEERS), tp),
        device_id_type=MESH,
    )

    def entering_copy(q):
        return pltpu.make_async_remote_copy(
            src_ref=en_out.at[q],
            dst_ref=en_in.at[mine],
            send_sem=en_send.at[q],
            recv_sem=en_recv,
            device_id=(group * PEERS + q, tp),
            device_id_type=MESH,
        )

    def sends(q):
        return jnp.logical_and(lax.rem(q, 2) == 0, group * PEERS + q > 0)

    def state_of(q):
        @pl.when(me != q)
        def _():
            pltpu.make_async_copy(st_in.at[q], st_in.at[q], st_recv.at[q]).wait()

        return st_in[q].astype(F32)

    def send_entering(q):
        @pl.when(sends(q))
        def _():
            entering_copy(q).start()

    @pl.when(group == 0)
    def _():
        pl.semaphore_wait(facing, 1)

    @pl.when(owns)
    def _():
        tot_in[me] = tot_out[mine]
        st_in[me] = st_out[mine]
        landed(tot_in, PEERS - 1, tot_recv)

    @pl.when(jnp.logical_and(owns, group == 0))
    def _():
        state = jnp.zeros((128, 128), F32)
        for q in range(PEERS):
            en_out[q] = state.astype(BF16)
            send_entering(q)
            state = tot_in[q][0:1] * state + state_of(q)
        half_out[...] = state.astype(BF16)

    @pl.when(jnp.logical_and(owns, group == 1))
    def _():
        state = jnp.zeros((128, 128), F32)
        left = jnp.ones((8, 128), F32)
        for q in range(PEERS):
            within[q] = state
            remains[q] = left
            state = tot_in[q][0:1] * state + state_of(q)
            left = tot_in[q] * left
        total_of_half.wait_recv()
        half = half_in[...].astype(F32)

        def body(i, c):
            q = 2 * jnp.where(place < 2, 3 - i, i)
            en_out[q] = (within[q] + remains[q][0:1] * half).astype(BF16)
            send_entering(q)
            return c

        lax.fori_loop(0, PEERS // 2, body, 0)

    @pl.when(jnp.logical_and(owns, group == 0))
    def _():
        total_of_half.start()

    weights[2].wait()
    acc_z[...] = jnp.zeros_like(acc_z)

    def gate(i, c):
        total = acc_z[...]
        for k in range(4):
            depth = pl.ds(pl.multiple_of((4 * i + k) * FEAT, FEAT), FEAT)
            total = total + dot(held[4 * i + k], vz[depth, :])
        acc_z[...] = total
        return c

    lax.fori_loop(0, 4, gate, 0)
    for t in range(LT):
        g = acc_z[:, t * 128 : (t + 1) * 128].astype(BF16).astype(F32)
        acc_z[:, t * 128 : (t + 1) * 128] = silu(g)

    @pl.when(ctx == 0)
    def _():
        en_in[...] = jnp.zeros_like(en_in)

    @pl.when(jnp.logical_and(ctx > 0, core == 0))
    def _():
        landed(en_in, 4, en_recv)

    @pl.when(core == 0)
    def _():
        pair_entering.start()

    @pl.when(owns)
    def _():
        pair_state.wait_recv()
        pair_total.wait_recv()
        pair_entering.wait_recv()
        for t in range(LT):
            passed = mate_tot[t][0:1] * en_in[t].astype(F32) + mate_st[t].astype(F32)
            en_in[t] = passed.astype(BF16)

    squares = jnp.zeros((ROWS, 128), F32)
    for t in range(LT):
        entering = en_in[t]
        gated = (y[t] + grow[t] * dot(bc[1], entering)) * acc_z[:, t * 128 : (t + 1) * 128]
        squares = squares + gated * gated
        y[t] = gated
    local = jnp.sum(squares.T, axis=0, keepdims=True)
    sq_out[...] = jnp.broadcast_to(local, (8, ROWS))
    norm = pltpu.make_async_remote_copy(
        src_ref=sq_out,
        dst_ref=sq_in,
        send_sem=sq_sem.at[0],
        recv_sem=sq_sem.at[1],
        device_id=(ctx, mate),
        device_id_type=MESH,
    )
    norm.start()
    norm.wait_recv()
    mean = (sq_out[0:1] + sq_in[0:1]) * (1.0 / (2 * LT * 128))
    scale = jnp.broadcast_to(lax.rsqrt(mean + 1e-5), (128, ROWS)).T
    for t in range(LT):
        cols = slice(t * 128, (t + 1) * 128)
        out[:, cols] = (y[t] * scale * gain[:, cols]).astype(BF16)

    norm.wait_send()
    most.wait_send()
    first_rows.wait_send()
    landed(held, 15, g_send)

    @pl.when(owns)
    def _():
        landed(tot_out, 3, tot_send)
        landed(st_out, 3, st_send)

    @pl.when(core == 0)
    def _():
        landed(tot_out, 4, tot_send)
        landed(st_out, 4, st_send)
        pair_state.wait_send()
        pair_total.wait_send()
        pair_entering.wait_send()

    @pl.when(ctx < SECTIONS - 1)
    def _():
        rim.wait_send()

    @pl.when(jnp.logical_and(owns, group == 0))
    def _():
        total_of_half.wait_send()

    for q in range(PEERS):

        @pl.when(jnp.logical_and(owns, sends(q)))
        def _(q=q):
            entering_copy(q).wait_send()


def local(tokens, w_z, w_x, w_bc, conv_x, conv_bc, bias_x, bias_bc, decay, step, skip, gain):
    hbm = pl.BlockSpec(memory_space=pl.ANY)
    vmem = pl.BlockSpec(memory_space=pltpu.VMEM)
    smem = pl.BlockSpec(memory_space=pltpu.SMEM)
    width = w_x.shape[1]
    dma = pltpu.SemaphoreType.DMA
    scratch = [
        pltpu.VMEM((16, ROWS, FEAT), BF16),
        pltpu.VMEM(w_z.shape, BF16),
        pltpu.VMEM(w_x.shape, BF16),
        pltpu.VMEM(w_bc.shape, BF16),
        pltpu.VMEM((ROWS, width), F32),
        pltpu.VMEM((ROWS, width), F32),
        pltpu.VMEM((ROWS, 128), F32),
        pltpu.VMEM((LT + 1, 8 + ROWS, 128), F32),
        pltpu.VMEM((LT + 1, 16, 128), BF16),
        pltpu.VMEM((LT + 1, 16, 128), BF16),
        pltpu.VMEM((LT, ROWS, 128), BF16),
        pltpu.VMEM((2, ROWS, 128), BF16),
        pltpu.VMEM((8, ROWS, ROWS), F32),
        pltpu.VMEM((LT, ROWS, 128), F32),
        pltpu.VMEM((LT, ROWS, 128), F32),
        pltpu.VMEM((LT, 8, 128), F32),
        pltpu.VMEM((PEERS, 8, 128), F32),
        pltpu.VMEM((LT, 128, 128), BF16),
        pltpu.VMEM((PEERS, 128, 128), BF16),
        pltpu.VMEM((PEERS, 128, 128), BF16),
        pltpu.VMEM((LT, 128, 128), BF16),
        pltpu.VMEM((128, 128), BF16),
        pltpu.VMEM((128, 128), BF16),
        pltpu.VMEM((PEERS, 128, 128), F32),
        pltpu.VMEM((PEERS, 8, 128), F32),
        pltpu.VMEM((LT, 128, 128), BF16),
        pltpu.VMEM((LT, 8, 128), F32),
        pltpu.VMEM((LT, ROWS, 128), F32),
        pltpu.VMEM((8, ROWS), F32),
        pltpu.VMEM((8, ROWS), F32),
        dma((3,)),
        dma,
        dma,
        dma((2, 16)),
        dma,
        dma,
        dma((2,)),
        dma((2, 2)),
        dma,
        dma((PEERS,)),
        dma((PEERS,)),
        dma,
        dma((2,)),
        dma((2,)),
        dma((2, 3)),
        pltpu.SemaphoreType.REGULAR,
        pltpu.SemaphoreType.REGULAR,
        pltpu.SemaphoreType.REGULAR,
    ]
    return pl.pallas_call(
        kernel,
        out_shape=pltpu.VMEM((ROWS, width), BF16),
        in_specs=[hbm] * 4 + [vmem] * 5 + [smem] * 2 + [vmem],
        out_specs=vmem,
        scratch_shapes=scratch,
        compiler_params=pltpu.CompilerParams(
            collective_id=0, has_side_effects=True, vmem_limit_bytes=56 * 2**20
        ),
    )(
        tokens, w_z, w_x, w_bc, conv_x, conv_bc, bias_x.reshape(1, -1), bias_bc.reshape(1, -1),
        decay.T, step, skip, gain.reshape(1, -1),
    )


def solution(mesh):
    return jax.shard_map(
        local,
        mesh=mesh,
        in_specs=(
            P("ctx", "tp"),
            P(None, "tp"),
            P(None, "tp"),
            P(None, "tp"),
            P(None, "tp"),
            P(None, "tp"),
            P("tp"),
            P("tp"),
            P("ctx", "tp"),
            P("tp"),
            P("tp"),
            P("tp"),
        ),
        out_specs=P("ctx", "tp"),
        check_vma=False,
    )
```

```python
import jax
import jax.numpy as jnp
from jax import lax
from jax.experimental import pallas as pl
from jax.experimental.pallas import tpu as pltpu
from jax.sharding import PartitionSpec as P

MESH = pl.DeviceIdType.MESH
SIDE = 4
TAPS = 4
ROWS = 256
HALF = 128
FEAT = 256
SECTIONS = 16
PEERS = 8
LT = 4
F32 = jnp.float32
BF16 = jnp.bfloat16


def silu(v):
    return v / (1.0 + jnp.exp(-v))


def dot(a, b, **kw):
    return jnp.dot(a, b, preferred_element_type=F32, **kw)


def kernel(
    tok, wz, wx, wbc, conv_x, conv_bc, bias_x, bias_bc, decay_t, step, skip, gain, out,
    held, vz, vx, vbc, acc_z, acc_x, acc_bc, pre, rim_out, rim_in, xs, bc, seg, grow, end_w,
    tot_out, tot_in, st_out, st_in, en_out, en_in, half_out, half_in, within, remains, mate_st, mate_tot, y, sq_out, sq_in,
    w_sem, own_sem, g_send, g_recv, tot_send, tot_recv, rim_sem, bc_sem, st_send, st_recv,
    en_send, en_recv, half_sem, sq_sem, pair_sem, up, down, facing,
):
    ctx, tp = lax.axis_index("ctx"), lax.axis_index("tp")
    core = lax.rem(ctx, 2)
    x, y_at = lax.div(tp, SIDE), lax.rem(tp, SIDE)

    def at(px, py):
        return lax.rem(px + 2 * SIDE, SIDE) * SIDE + lax.rem(py + 2 * SIDE, SIDE)

    mate = at(x, y_at + 1 - 2 * lax.rem(y_at, 2))
    z = lax.div(ctx, 2)
    group, me = lax.div(ctx, PEERS), lax.rem(ctx, PEERS)
    place = lax.rem(z, 4)
    far_place = lax.rem(place + 2, 4)
    facing_at = ((1 - group) * 4 + far_place) * 2 + core

    mine = lax.rem(place + 2 * group, 4)
    owns = core == 1

    def signal(sem, section, column=None):
        pl.semaphore_signal(
            sem, inc=1, device_id=(section, tp if column is None else column), device_id_type=MESH
        )

    barrier = pltpu.get_barrier_semaphore()
    for px, py in ((1, 0), (-1, 0), (0, 1), (0, -1), (2, 0), (0, 2)):
        signal(barrier, ctx, at(x + px, y_at + py))
    signal(barrier, ctx + 1 - 2 * core)

    @pl.when(z < 7)
    def _():
        signal(barrier, ctx + 2)

    @pl.when(group == 0)
    def _():
        signal(barrier, facing_at)

    weights = [
        pltpu.make_async_copy(a, b, w_sem.at[i])
        for i, (a, b) in enumerate(((wx, vx), (wbc, vbc), (wz, vz)))
    ]
    own = pltpu.make_async_copy(tok, held.at[tp], own_sem)
    own.start()
    for w in weights:
        w.start()
    pl.semaphore_wait(barrier, 7 + lax.min(z, 1) + group)

    def slot(dx, dy):
        return at(x - dx, y_at - dy)

    def piece(s, half):
        return held.at[s, pl.ds(half * HALF, HALF), :]

    def dxy(half, first, second):
        return (second, first) if half == 0 else (first, second)

    def send(half, source, direction, along, landing):
        dx, dy = dxy(half, *source)
        px, py = dxy(half, *((direction, 0) if along == 0 else (0, direction)))
        first, second = landing
        s = slot(dx, dy)
        src = tok.at[pl.ds(half * HALF, HALF), :] if all(isinstance(v, int) and v == 0 for v in source) else piece(s, half)
        pltpu.make_async_remote_copy(
            src_ref=src,
            dst_ref=piece(s, half),
            send_sem=g_send,
            recv_sem=g_recv.at[half, first * SIDE + second],
            device_id=(ctx, at(x + px, y_at + py)),
            device_id_type=MESH,
        ).start()

    def arrived(half, first, second):
        p = piece(slot(*dxy(half, first, second)), half)
        pltpu.make_async_copy(p, p, g_recv.at[half, first * SIDE + second]).wait()

    def along_second(half, first):
        send(half, (first, 0), 1, 1, (first, 1))
        send(half, (first, 0), -1, 1, (first, 3))

    def across_second(half, first):
        flag = lax.rem(first + core, 2)

        send(half, (first, 1 + 2 * flag), 1 - 2 * flag, 1, (first, 2))

    def multiply(dx, dy, begin=False):
        s = slot(dx, dy)
        a = held[s]
        depth = pl.ds(pl.multiple_of(s * FEAT, FEAT), FEAT)
        for acc, v in ((acc_x, vx), (acc_bc, vbc)):
            part = dot(a, v[depth, :])
            acc[...] = part if begin else acc[...] + part

    def multiply_all(count, offsets):
        def body(i, c):
            multiply(*offsets(i))
            return c

        lax.fori_loop(0, count, body, 0)

    for half in (0, 1):
        send(half, (0, 0), 2, 0, (2, 0))
    for half in (0, 1):
        send(half, (0, 0), 1, 0, (1, 0))
        send(half, (0, 0), -1, 0, (3, 0))
    for half in (0, 1):
        along_second(half, 0)

    @pl.when(group == 1)
    def _():
        signal(facing, facing_at)

    @pl.when(place == 3)
    def _():
        signal(up, ctx - 2)

    def sweep_up(at_place):
        @pl.when(place == at_place)
        def _():
            pl.semaphore_wait(up, 1)
            if at_place == 0:
                signal(down, ctx + 2)

        @pl.when(jnp.logical_and(place == at_place, z > 0))
        def _():
            signal(up, ctx - 2)

    def sweep_down(at_place):
        @pl.when(place == at_place)
        def _():
            pl.semaphore_wait(down, 1)
            if at_place < 3:
                signal(down, ctx + 2)

    i0 = lax.broadcasted_iota(jnp.int32, (ROWS, ROWS), 0)
    i1 = lax.broadcasted_iota(jnp.int32, (ROWS, ROWS), 1)
    upper = (i0 <= i1).astype(F32)
    cum_t = dot(decay_t[...], upper, precision=lax.Precision.HIGHEST)
    lane = lax.broadcasted_iota(jnp.int32, (1, 128), 1)
    for t in range(LT):
        rows = jnp.concatenate(
            [jnp.broadcast_to(cum_t[2 * t + k : 2 * t + k + 1], (64, ROWS)) for k in (0, 1)], 0
        )
        cum = rows.T
        total = cum[ROWS - 1 : ROWS]
        step_row = jnp.where(lane < 64, step[2 * t], step[2 * t + 1])
        grow[t] = jnp.exp(cum)
        end_w[t] = jnp.exp(total - cum) * step_row
        tot_out[t] = jnp.broadcast_to(jnp.exp(total), (8, 128))

    for half in (0, 1):
        arrived(half, 2, 0)
        along_second(half, 2)
    for half in (0, 1):
        arrived(half, 1, 0)
        along_second(half, 1)
        arrived(half, 3, 0)
        along_second(half, 3)
    for h in range(8):
        if h == 4:
            for half in (0, 1):
                arrived(half, 0, 1)
                arrived(half, 0, 3)
                across_second(half, 0)
        row = cum_t[h : h + 1]
        col = jnp.broadcast_to(row, (128, ROWS)).T
        col = jnp.concatenate([col, col], axis=1)
        keep = i0 >= i1
        seg[h] = jnp.where(keep, jnp.exp(jnp.where(keep, col - row, 0.0)), 0.0) * step[h]

    for half in (0, 1):
        arrived(half, 2, 1)
        arrived(half, 2, 3)
        across_second(half, 2)
    own.wait()
    weights[0].wait()
    weights[1].wait()
    multiply(0, 0, True)

    def beside(i):
        o, swap = 1 + 2 * lax.rem(i, 2), lax.div(i, 2)
        return swap * o, (1 - swap) * o

    multiply_all(4, beside)
    sweep_up(2)
    for half in (0, 1):
        arrived(half, 1, 1)
        arrived(half, 1, 3)
        across_second(half, 1)
    for half in (0, 1):
        arrived(half, 3, 1)
        arrived(half, 3, 3)
        across_second(half, 3)
    sweep_up(1)
    multiply_all(4, lambda i: (1 + 2 * lax.rem(i, 2), 1 + 2 * lax.div(i, 2)))
    sweep_up(0)
    for half in (0, 1):
        arrived(half, 0, 2)
    multiply_all(2, lambda i: (2 * (1 - i), 2 * i))
    sweep_down(1)
    for half in (0, 1):
        arrived(half, 1, 2)
        arrived(half, 3, 2)

    def far(i):
        o, swap = 1 + 2 * lax.rem(i, 2), lax.div(i, 2)
        return o + swap * (2 - o), 2 + swap * (o - 2)

    multiply_all(4, far)
    sweep_down(2)
    for half in (0, 1):
        arrived(half, 2, 2)
    multiply(2, 2)
    sweep_down(3)

    def before_conv(t, rows):
        p = acc_bc[rows] if t == LT else acc_x[rows, t * 128 : (t + 1) * 128]
        return p.astype(BF16)

    for t in range(LT + 1):
        rim_out[t] = before_conv(t, slice(ROWS - 16, ROWS))
    rim = pltpu.make_async_remote_copy(
        src_ref=rim_out,
        dst_ref=rim_in,
        send_sem=rim_sem.at[0],
        recv_sem=rim_sem.at[1],
        device_id=(lax.min(ctx + 1, SECTIONS - 1), tp),
        device_id_type=MESH,
    )

    @pl.when(z == 3)
    def _():
        pl.semaphore_wait(up, 1)

    @pl.when(ctx < SECTIONS - 1)
    def _():
        rim.start()

    for t in range(LT + 1):
        pre[t, 8 : 8 + ROWS] = before_conv(t, slice(0, ROWS)).astype(F32)
    def to_owners(send_one):
        def body(i, c):
            p = lax.rem(place + i, 4)
            send_one(lax.rem(p + 2 * group, 4), group * PEERS + 2 * p + 1)
            return c

        lax.fori_loop(1, 4, body, 0)

        @pl.when(core == 0)
        def _():
            send_one(mine, ctx + 1)

    def send_total(piece_of, section):
        pltpu.make_async_remote_copy(
            src_ref=tot_out.at[piece_of],
            dst_ref=tot_in.at[me],
            send_sem=tot_send,
            recv_sem=tot_recv,
            device_id=(section, tp),
            device_id_type=MESH,
        ).start()

    def send_state(piece_of, section):
        pltpu.make_async_remote_copy(
            src_ref=st_out.at[piece_of],
            dst_ref=st_in.at[me],
            send_sem=st_send,
            recv_sem=st_recv.at[me],
            device_id=(section, tp),
            device_id_type=MESH,
        ).start()

    def conv(t, low, high):
        cols = slice(0, 128) if t == LT else slice(t * 128, (t + 1) * 128)
        taps, bias = (conv_bc, bias_bc) if t == LT else (conv_x, bias_x)
        total = bias[:, cols] + jnp.zeros((high - low, 128), F32)
        for k in range(TAPS):
            total = total + taps[k : k + 1, cols] * pre[t, 5 + k + low : 5 + k + high]
        return silu(total).astype(BF16)

    side = lax.rem(tp, 2)

    def swap(which, low, high):
        part = bc.at[side, pl.ds(low, high - low)]
        return pltpu.make_async_remote_copy(
            src_ref=part,
            dst_ref=part,
            send_sem=bc_sem.at[0, which],
            recv_sem=bc_sem.at[1, which],
            device_id=(ctx, mate),
            device_id_type=MESH,
        )

    most, first_rows = swap(0, 16, ROWS), swap(1, 0, 16)
    bc[side, 16:ROWS] = conv(LT, 16, ROWS)
    most.start()
    for t in range(LT):
        xs[t, 16:ROWS] = conv(t, 16, ROWS)
    to_owners(send_total)

    @pl.when(ctx == 0)
    def _():
        rim_in[...] = jnp.zeros_like(rim_in)

    @pl.when(ctx > 0)
    def _():
        rim.wait_recv()

    for t in range(LT + 1):
        pre[t, 0:8] = rim_in[t].astype(F32)[8:]
    bc[side, 0:16] = conv(LT, 0, 16)
    first_rows.start()
    for t in range(LT):
        xs[t, 0:16] = conv(t, 0, 16)
    for which, low, high in ((0, 16, ROWS), (1, 0, 16)):
        other = bc.at[1 - side, pl.ds(low, high - low)]
        pltpu.make_async_copy(other, other, bc_sem.at[1, which]).wait()

    b_t = bc[0].astype(F32).T.astype(BF16)
    for t in range(LT):
        weighted = (xs[t].astype(F32) * end_w[t]).astype(BF16)
        st_out[t] = dot(b_t, weighted).astype(BF16)
    to_owners(send_state)

    def to_pair(src, dst, which):
        return pltpu.make_async_remote_copy(
            src_ref=src,
            dst_ref=dst,
            send_sem=pair_sem.at[0, which],
            recv_sem=pair_sem.at[1, which],
            device_id=(ctx + 1 - 2 * core, tp),
            device_id_type=MESH,
        )

    pair_state = to_pair(st_out, mate_st, 0)
    pair_total = to_pair(tot_out, mate_tot, 1)
    pair_entering = to_pair(en_in, en_in, 2)

    @pl.when(core == 0)
    def _():
        pair_state.start()
        pair_total.start()


    scores = dot(bc[1], b_t)

    def intra(t):
        both = [dot((seg[2 * t + k] * scores).astype(BF16), xs[t]) for k in (0, 1)]
        skip_row = jnp.where(lane < 64, skip[2 * t], skip[2 * t + 1])
        y[t] = jnp.where(lane < 64, both[0], both[1]) + skip_row * xs[t].astype(F32)

    for t in range(LT):
        intra(t)

    def landed(ref, count, sem):
        part = ref.at[pl.ds(0, count)]
        pltpu.make_async_copy(part, part, sem).wait()

    total_of_half = pltpu.make_async_remote_copy(
        src_ref=half_out,
        dst_ref=half_in,
        send_sem=half_sem.at[0],
        recv_sem=half_sem.at[1],
        device_id=(lax.max(facing_at, PEERS), tp),
        device_id_type=MESH,
    )

    def entering_copy(q):
        return pltpu.make_async_remote_copy(
            src_ref=en_out.at[q],
            dst_ref=en_in.at[mine],
            send_sem=en_send.at[q],
            recv_sem=en_recv,
            device_id=(group * PEERS + q, tp),
            device_id_type=MESH,
        )

    def sends(q):
        return jnp.logical_and(lax.rem(q, 2) == 0, group * PEERS + q > 0)

    def state_of(q):
        @pl.when(me != q)
        def _():
            pltpu.make_async_copy(st_in.at[q], st_in.at[q], st_recv.at[q]).wait()

        return st_in[q].astype(F32)

    def send_entering(q):
        @pl.when(sends(q))
        def _():
            entering_copy(q).start()

    @pl.when(group == 0)
    def _():
        pl.semaphore_wait(facing, 1)

    @pl.when(owns)
    def _():
        tot_in[me] = tot_out[mine]
        st_in[me] = st_out[mine]
        landed(tot_in, PEERS - 1, tot_recv)

    @pl.when(jnp.logical_and(owns, group == 0))
    def _():
        state = jnp.zeros((128, 128), F32)
        for q in range(PEERS):
            en_out[q] = state.astype(BF16)
            send_entering(q)
            state = tot_in[q][0:1] * state + state_of(q)
        half_out[...] = state.astype(BF16)

    @pl.when(jnp.logical_and(owns, group == 1))
    def _():
        state = jnp.zeros((128, 128), F32)
        left = jnp.ones((8, 128), F32)
        for q in range(PEERS):
            within[q] = state
            remains[q] = left
            state = tot_in[q][0:1] * state + state_of(q)
            left = tot_in[q] * left
        total_of_half.wait_recv()
        half = half_in[...].astype(F32)

        def body(i, c):
            q = 2 * jnp.where(place < 2, 3 - i, i)
            en_out[q] = (within[q] + remains[q][0:1] * half).astype(BF16)
            send_entering(q)
            return c

        lax.fori_loop(0, PEERS // 2, body, 0)

    @pl.when(jnp.logical_and(owns, group == 0))
    def _():
        total_of_half.start()

    weights[2].wait()
    acc_z[...] = jnp.zeros_like(acc_z)

    def gate(i, c):
        total = acc_z[...]
        for k in range(4):
            depth = pl.ds(pl.multiple_of((4 * i + k) * FEAT, FEAT), FEAT)
            total = total + dot(held[4 * i + k], vz[depth, :])
        acc_z[...] = total
        return c

    lax.fori_loop(0, 4, gate, 0)
    for t in range(LT):
        g = acc_z[:, t * 128 : (t + 1) * 128].astype(BF16).astype(F32)
        acc_z[:, t * 128 : (t + 1) * 128] = silu(g)

    @pl.when(ctx == 0)
    def _():
        en_in[...] = jnp.zeros_like(en_in)

    @pl.when(jnp.logical_and(ctx > 0, core == 0))
    def _():
        landed(en_in, 4, en_recv)

    @pl.when(core == 0)
    def _():
        pair_entering.start()

    @pl.when(owns)
    def _():
        pair_state.wait_recv()
        pair_total.wait_recv()
        pair_entering.wait_recv()
        for t in range(LT):
            passed = mate_tot[t][0:1] * en_in[t].astype(F32) + mate_st[t].astype(F32)
            en_in[t] = passed.astype(BF16)

    squares = jnp.zeros((ROWS, 128), F32)
    for t in range(LT):
        entering = en_in[t]
        gated = (y[t] + grow[t] * dot(bc[1], entering)) * acc_z[:, t * 128 : (t + 1) * 128]
        squares = squares + gated * gated
        y[t] = gated
    local = jnp.sum(squares.T, axis=0, keepdims=True)
    sq_out[...] = jnp.broadcast_to(local, (8, ROWS))
    norm = pltpu.make_async_remote_copy(
        src_ref=sq_out,
        dst_ref=sq_in,
        send_sem=sq_sem.at[0],
        recv_sem=sq_sem.at[1],
        device_id=(ctx, mate),
        device_id_type=MESH,
    )
    norm.start()
    norm.wait_recv()
    mean = (sq_out[0:1] + sq_in[0:1]) * (1.0 / (2 * LT * 128))
    scale = jnp.broadcast_to(lax.rsqrt(mean + 1e-5), (128, ROWS)).T
    for t in range(LT):
        cols = slice(t * 128, (t + 1) * 128)
        out[:, cols] = (y[t] * scale * gain[:, cols]).astype(BF16)

    norm.wait_send()
    most.wait_send()
    first_rows.wait_send()
    landed(held, 15, g_send)

    @pl.when(owns)
    def _():
        landed(tot_out, 3, tot_send)
        landed(st_out, 3, st_send)

    @pl.when(core == 0)
    def _():
        landed(tot_out, 4, tot_send)
        landed(st_out, 4, st_send)
        pair_state.wait_send()
        pair_total.wait_send()
        pair_entering.wait_send()

    @pl.when(ctx < SECTIONS - 1)
    def _():
        rim.wait_send()

    @pl.when(jnp.logical_and(owns, group == 0))
    def _():
        total_of_half.wait_send()

    for q in range(PEERS):

        @pl.when(jnp.logical_and(owns, sends(q)))
        def _(q=q):
            entering_copy(q).wait_send()


def local(tokens, w_z, w_x, w_bc, conv_x, conv_bc, bias_x, bias_bc, decay, step, skip, gain):
    hbm = pl.BlockSpec(memory_space=pl.ANY)
    vmem = pl.BlockSpec(memory_space=pltpu.VMEM)
    smem = pl.BlockSpec(memory_space=pltpu.SMEM)
    width = w_x.shape[1]
    dma = pltpu.SemaphoreType.DMA
    scratch = [
        pltpu.VMEM((16, ROWS, FEAT), BF16),
        pltpu.VMEM(w_z.shape, BF16),
        pltpu.VMEM(w_x.shape, BF16),
        pltpu.VMEM(w_bc.shape, BF16),
        pltpu.VMEM((ROWS, width), F32),
        pltpu.VMEM((ROWS, width), F32),
        pltpu.VMEM((ROWS, 128), F32),
        pltpu.VMEM((LT + 1, 8 + ROWS, 128), F32),
        pltpu.VMEM((LT + 1, 16, 128), BF16),
        pltpu.VMEM((LT + 1, 16, 128), BF16),
        pltpu.VMEM((LT, ROWS, 128), BF16),
        pltpu.VMEM((2, ROWS, 128), BF16),
        pltpu.VMEM((8, ROWS, ROWS), F32),
        pltpu.VMEM((LT, ROWS, 128), F32),
        pltpu.VMEM((LT, ROWS, 128), F32),
        pltpu.VMEM((LT, 8, 128), F32),
        pltpu.VMEM((PEERS, 8, 128), F32),
        pltpu.VMEM((LT, 128, 128), BF16),
        pltpu.VMEM((PEERS, 128, 128), BF16),
        pltpu.VMEM((PEERS, 128, 128), BF16),
        pltpu.VMEM((LT, 128, 128), BF16),
        pltpu.VMEM((128, 128), BF16),
        pltpu.VMEM((128, 128), BF16),
        pltpu.VMEM((PEERS, 128, 128), F32),
        pltpu.VMEM((PEERS, 8, 128), F32),
        pltpu.VMEM((LT, 128, 128), BF16),
        pltpu.VMEM((LT, 8, 128), F32),
        pltpu.VMEM((LT, ROWS, 128), F32),
        pltpu.VMEM((8, ROWS), F32),
        pltpu.VMEM((8, ROWS), F32),
        dma((3,)),
        dma,
        dma,
        dma((2, 16)),
        dma,
        dma,
        dma((2,)),
        dma((2, 2)),
        dma,
        dma((PEERS,)),
        dma((PEERS,)),
        dma,
        dma((2,)),
        dma((2,)),
        dma((2, 3)),
        pltpu.SemaphoreType.REGULAR,
        pltpu.SemaphoreType.REGULAR,
        pltpu.SemaphoreType.REGULAR,
    ]
    return pl.pallas_call(
        kernel,
        out_shape=pltpu.VMEM((ROWS, width), BF16),
        in_specs=[hbm] * 4 + [vmem] * 5 + [smem] * 2 + [vmem],
        out_specs=vmem,
        scratch_shapes=scratch,
        compiler_params=pltpu.CompilerParams(
            collective_id=0, has_side_effects=True, vmem_limit_bytes=56 * 2**20
        ),
    )(
        tokens, w_z, w_x, w_bc, conv_x, conv_bc, bias_x.reshape(1, -1), bias_bc.reshape(1, -1),
        decay.T, step, skip, gain.reshape(1, -1),
    )


def solution(mesh):
    return jax.shard_map(
        local,
        mesh=mesh,
        in_specs=(
            P("ctx", "tp"),
            P(None, "tp"),
            P(None, "tp"),
            P(None, "tp"),
            P(None, "tp"),
            P(None, "tp"),
            P("tp"),
            P("tp"),
            P("ctx", "tp"),
            P("tp"),
            P("tp"),
            P("tp"),
        ),
        out_specs=P("ctx", "tp"),
        check_vma=False,
    )
```
